128 devices in a mesh: row: 8 (over y_hi, z), col: 16 (over x, y_lo, core).
Axes of the slice: x: 4, y: 4 (y_hi: 2, y_lo: 2; y = y_hi * 2 + y_lo), z: 4, core: 2. Of those that a mesh axis runs over, the one named last changes fastest.
Arguments:
- strain: bfloat16 [2048, 33280], P(('row', 'col')), may hold values from -6 to 6
- file_channels: int32 [2048], P(('row', 'col')), may hold values from 0 to 511, as said below
- file_counts: int32 [128], P(('row', 'col')), may hold values from 0 to 16, as said below
- window_start: int32 [128], P(('row', 'col')), may hold values from 0 to 512
Outputs:
- correlations: bfloat16 [512, 512, 1024], P('row', 'col')
The draws below stay inside these ranges and needn't reach their ends.
Inputs may be any that keep to these rules, and one draw needn't show every extreme that they name: `file_channels`: the first file_counts[d] slots of file d are live. The live slots of the 8 files with one col index hold, each exactly once, the channels g whose owner ((g // 4) // 16, (g // 4) % 16) has that col index; dead slots hold arbitrary channel numbers. One file holds at most 2 channels of one owner, and exactly 2 for some file and owner in every group of files with one col index. `file_counts`: in every group of files with one col index some file has all 16 slots live.
All inputs are finite; a program needn't handle non-finite values.
Results may differ from the reference program's by a relative error of at most 0.0076.
Values may be sent and summed in bfloat16 or wider, within the bound.
No kernel may reach another device: no remote copies, remote signals or barrier semaphores. Data moves between devices by JAX's collectives and lax.ppermute only.
A program may use at most 128 MiB of HBM per device.

```python
import math
import jax
import jax.numpy as jnp
from jax import lax

NF = 2048
NT = 4096
LAGS = 1024
SEGS = 8
CH_DEV = 4
CAP = 2
SPAN = 512
SMOOTH = 32
EDGE = 128
SLOTS = 16
NCH = 512
TFILE = 33280
N_ROW = 8
N_COL = 16
DEVICES = 128


def file_layout(key):
    layout_key = jax.random.fold_in(key, 11)
    column_keys = jax.random.split(layout_key, N_COL)

    def one_column(column_key, column):
        sub_keys = jax.random.split(column_key, 5)
        file_order = jax.random.permutation(sub_keys[0], N_ROW)
        offsets = jax.random.randint(sub_keys[2], (N_ROW,), 0, N_ROW - 1)
        owners = jnp.repeat(jnp.arange(N_ROW, dtype=jnp.int32), CH_DEV)
        within = jnp.tile(jnp.arange(CH_DEV, dtype=jnp.int32), N_ROW)
        hot_pair = within < CAP
        spread = within - CAP
        position = jnp.where(hot_pair, 0, 1 + jnp.mod(offsets[owners] + spread, N_ROW - 1))
        file_of = file_order[position].astype(jnp.int32)
        channels = ((owners * N_COL + column) * CH_DEV + within).astype(jnp.int32)
        item_count = N_ROW * CH_DEV
        ranking = jax.random.permutation(sub_keys[3], item_count).astype(jnp.int32)
        sorted_index = jnp.argsort(file_of * item_count + ranking, stable=True)
        sorted_files = file_of[sorted_index]
        counts = jnp.sum((file_of[None, :] == jnp.arange(N_ROW, dtype=jnp.int32)[:, None]).astype(jnp.int32), axis=1)
        starts = jnp.cumsum(counts) - counts
        slot_of = jnp.arange(item_count, dtype=jnp.int32) - starts[sorted_files]
        filler = jax.random.randint(sub_keys[4], (N_ROW, SLOTS), 0, NCH)
        slot_table = filler.at[sorted_files, slot_of].set(channels[sorted_index])
        return (slot_table.astype(jnp.int32), counts.astype(jnp.int32))
    tables, counts = jax.vmap(one_column)(column_keys, jnp.arange(N_COL, dtype=jnp.int32))
    return (jnp.transpose(tables, (1, 0, 2)).reshape(-1), jnp.transpose(counts).reshape(-1))


def draw_file_channels(key, part):
    return file_layout(key)[0]


def draw_file_counts(key, part):
    return file_layout(key)[1]


def touch_ends(drawn, own_key, least, high):
    place = [jax.random.randint(jax.random.fold_in(own_key, axis), (), 0, length) for axis, length in enumerate(drawn.shape)]
    main_axis = drawn.shape.index(max(drawn.shape))
    neighbour = place[:main_axis] + [(place[main_axis] + 1) % drawn.shape[main_axis]] + place[main_axis + 1:]
    return drawn.at[tuple(place)].set(least).at[tuple(neighbour)].set(high)


def level_of(key, dims, pieces, smallest, largest):
    loudness, own = 1.0, jax.random.fold_in(key, 6)
    for dim, shards_of in pieces:
        draws = jnp.exp(jax.random.uniform(jax.random.fold_in(own, dim), (shards_of,), jnp.float32, smallest / len(pieces), largest / len(pieces)))
        loudness = loudness * jnp.repeat(draws, dims[dim] // shards_of).reshape([-1 if axis == dim else 1 for axis in range(len(dims))])
    return loudness


def bell_draw(key, shape, scale, bound, shards=(), kind=jnp.bfloat16):
    values = jax.random.normal(key, shape, jnp.float32) * scale
    if len(shards) > 0:
        values = level_of(key, shape, shards, -0.22, 0.18) * values
    return jnp.clip(values, min=-bound, max=bound).astype(kind)


def setup_inputs(seed: int = 0) -> dict:
    key_list = jax.random.split(jax.random.key(seed), 5)
    strain = bell_draw(key_list[0], (DEVICES * SLOTS, TFILE), 1.0, 6.0, ((0, 128),))
    file_channels = draw_file_channels(jax.random.fold_in(key_list[4], 71), 0)
    file_counts = draw_file_counts(jax.random.fold_in(key_list[4], 71), 0)
    window_start = touch_ends(jax.random.randint(key_list[3], (DEVICES,), 0, SPAN + 1), jax.random.fold_in(key_list[3], 1), 0, SPAN).astype(jnp.int32)
    return {"strain": strain, "file_channels": file_channels, "file_counts": file_counts, "window_start": window_start}


def dft_block(first_freq, freq_count, length):
    sample_index = jnp.arange(length, dtype=jnp.int32)[:, None]
    freq_index = first_freq + jnp.arange(freq_count, dtype=jnp.int32)[None, :]
    phases = jnp.mod(sample_index * freq_index, length).astype(jnp.float32) * (2.0 * math.pi / length)
    return jnp.concatenate([jnp.cos(phases), -jnp.sin(phases)], axis=1).astype(jnp.bfloat16)

def lag_table():
    freq_index = jnp.arange(NF, dtype=jnp.int32)[:, None]
    lag_index = jnp.arange(LAGS, dtype=jnp.int32)[None, :] - LAGS // 2
    phases = jnp.mod(freq_index * lag_index, NT).astype(jnp.float32) * (2.0 * math.pi / NT)
    return jnp.concatenate([jnp.cos(phases), -jnp.sin(phases)], axis=0).astype(jnp.bfloat16)

def band_taper(freq_count):
    freq_index = jnp.arange(freq_count, dtype=jnp.float32)
    distance = jnp.minimum(freq_index + 0.5, freq_count - freq_index - 0.5)
    rising = jnp.minimum(distance / EDGE, 1.0)
    return jnp.sin(0.5 * math.pi * rising) ** 2

def whiten(real_part, imag_part):
    powers = real_part * real_part + imag_part * imag_part
    padded = jnp.pad(powers, ((0, 0), (SMOOTH + 1, SMOOTH)))
    running = jnp.cumsum(padded, axis=1)
    window_sum = running[:, 2 * SMOOTH + 1:] - running[:, :powers.shape[1]]
    scaling = band_taper(powers.shape[1])[None, :] / jnp.sqrt(window_sum / (2 * SMOOTH + 1) + 1e-06)
    return (real_part * scaling, imag_part * scaling)

def reference(strain, file_channels, file_counts, window_start):
    file_total = file_counts.shape[0]
    file_blocks = strain.reshape(file_total, SLOTS, strain.shape[1])

    def cut_window(block, first_sample):
        return lax.dynamic_slice_in_dim(block, first_sample, SEGS * NT, 1)
    windows = jax.vmap(cut_window)(file_blocks, window_start).reshape(file_total * SLOTS, SEGS * NT)
    live_slot = (jnp.arange(SLOTS, dtype=jnp.int32)[None, :] < file_counts[:, None]).reshape(-1)
    target = jnp.where(live_slot, file_channels, NCH).astype(jnp.int32)
    traces = jnp.zeros((NCH + 1, SEGS * NT), jnp.bfloat16).at[target].set(windows)[:NCH]
    segment_rows = traces.reshape(NCH * SEGS, NT).astype(jnp.float32)
    table = dft_block(jnp.int32(0), NF, NT).astype(jnp.float32)
    product = jnp.dot(segment_rows, table, precision=lax.Precision.HIGHEST)
    real_part, imag_part = whiten(product[:, :NF], product[:, NF:])
    spectra = jnp.stack([real_part.reshape(NCH, SEGS, NF), imag_part.reshape(NCH, SEGS, NF)], axis=1).astype(jnp.bfloat16)
    spectra = lax.optimization_barrier(spectra).astype(jnp.float32)
    column = jnp.arange(NCH, dtype=jnp.int32)
    group_size = N_ROW * CH_DEV
    col_ids = (column % group_size // CH_DEV * N_COL + column // group_size) * CH_DEV + column % CH_DEV
    col_spectra = spectra[col_ids]
    flipped = jnp.concatenate([-col_spectra[:, 1:2], col_spectra[:, 0:1]], axis=1)
    inverse = lag_table().astype(jnp.float32)
    norm_scale = 1.0 / math.sqrt(SEGS * NF)

    def one_block(block_index):
        first_row = block_index * 8
        row_block = lax.dynamic_slice_in_dim(spectra, first_row, 8, 0)
        real_cross = jnp.einsum('icsf,jcsf->ijf', row_block, col_spectra, precision=lax.Precision.HIGHEST)
        imag_cross = jnp.einsum('icsf,jcsf->ijf', row_block, flipped, precision=lax.Precision.HIGHEST)
        cross = jnp.concatenate([real_cross, imag_cross], axis=2).astype(jnp.bfloat16)
        cross = lax.optimization_barrier(cross).astype(jnp.float32)
        lagged = jnp.dot(cross.reshape(8 * NCH, 2 * NF), inverse, precision=lax.Precision.HIGHEST).reshape(8, NCH, LAGS)
        row_ids = first_row + jnp.arange(8, dtype=jnp.int32)
        keep_pair = (row_ids[:, None] != col_ids[None, :]).astype(jnp.float32)
        return (lagged * (keep_pair[:, :, None] * norm_scale)).astype(jnp.bfloat16)
    blocks_out = lax.map(one_block, jnp.arange(NCH // 8, dtype=jnp.int32))
    return blocks_out.reshape(NCH, NCH, LAGS)
```

```python
import functools
import math

import jax
import jax.numpy as jnp
import numpy as np
from jax import lax
from jax.experimental import pallas as pl
from jax.experimental.pallas import tpu as pltpu
from jax.sharding import PartitionSpec as P

NF = 2048
NT = 4096
LAGS = 1024
SEGS = 8
CH = 4
SLOTS = 16
SMOOTH = 32
EDGE = 128
WIN = SEGS * NT
HALF = NF // 2
GRP = 16
NGRP = HALF // GRP
BF = jnp.bfloat16
F32 = jnp.float32


def frequency_order():
    p = np.arange(HALF).reshape(NGRP, 1, GRP)
    mirror = np.where(p == 0, HALF, NF - p)
    return np.concatenate([p, mirror], axis=1).reshape(NF)


def trig(product, size):
    angle = (product % size).astype(np.float32) * np.float32(2.0 * math.pi / size)
    return np.cos(angle.astype(np.float64)), -np.sin(angle.astype(np.float64))


@functools.cache
def dft_table():
    order = frequency_order().astype(np.int64)
    cos, sin = trig(np.arange(NT, dtype=np.int64)[:, None] * order[None, :], NT)
    both = np.stack([cos.reshape(NT, 8, 256), sin.reshape(NT, 8, 256)], axis=2)
    return both.transpose(1, 0, 2, 3).reshape(8, NT, 512).astype(jnp.bfloat16)


@functools.cache
def smooth_table():
    order = frequency_order()
    near = np.abs(order[:, None] - order[None, :]) <= SMOOTH
    tiles = NF // 128
    out = np.zeros((tiles, 3, 128, 128), np.float32)
    for t in range(tiles):
        for k in range(3):
            s = (t + k - 1) % tiles
            out[t, k] = near[s * 128 : s * 128 + 128, t * 128 : t * 128 + 128]
    assert out.sum() == near.sum()
    return out.reshape(tiles, 384, 128).astype(jnp.bfloat16)


@functools.cache
def taper_row():
    f = frequency_order().astype(np.float64)
    rising = np.minimum(np.minimum(f + 0.5, NF - f - 0.5) / EDGE, 1.0)
    return (np.sin(0.5 * math.pi * rising) ** 2).astype(np.float32).reshape(1, NF)


@functools.cache
def spread_table():
    lane = np.arange(128)
    out = np.zeros((128, 8, 128), np.float32)
    for u in range(8):
        out[:, u] = (lane[:, None] // 16 == u) & (lane[:, None] % 16 == lane[None, :] % 16)
    return out.reshape(128, 1024).astype(jnp.bfloat16)


@functools.cache
def lag_tables():
    p = np.arange(HALF, dtype=np.int64)
    out = np.zeros((4, LAGS // 2, HALF), np.float32)
    for odd in range(2):
        m = np.arange(odd, LAGS, 2, dtype=np.int64) - LAGS // 2
        cos, sin = trig(m[:, None] * p[None, :], NT)
        mid_cos, mid_sin = trig(m * HALF, NT)
        out[2 * odd], out[2 * odd + 1] = cos, sin
        out[2 * odd + 1, :, 0] = np.rint(mid_sin if odd else mid_cos)
    return out.astype(jnp.bfloat16)


def spectra_kernel(pick_ref, got_ref, smooth_ref, taper_ref, spread_ref, table_ref, out_ref, x_ref, re_ref, im_ref):
    step = pl.program_id(0)

    @pl.when(step == 0)
    def _():
        for s in range(SEGS):
            seg = got_ref[:, s * NT : (s + 1) * NT]
            x = jnp.dot(pick_ref[...], seg, preferred_element_type=F32)
            x_ref[s * 8 : s * 8 + 8, :] = x

    prod = jnp.dot(x_ref[...].astype(BF), table_ref[0], preferred_element_type=F32)
    cols = pl.ds(pl.multiple_of(step * 256, 256), 256)
    re_ref[:, cols] = prod[:, :256]
    im_ref[:, cols] = prod[:, 256:]

    @pl.when(step == pl.num_programs(0) - 1)
    def _():
        tiles = NF // 128

        def power(t):
            lanes = slice(t % tiles * 128, t % tiles * 128 + 128)
            re, im = re_ref[:, lanes], im_ref[:, lanes]
            p = re * re + im * im
            hi = p.astype(BF)
            return jnp.concatenate([hi, (p - hi.astype(F32)).astype(BF)], axis=0)

        powers = [power(t) for t in range(tiles)]
        row = lax.broadcasted_iota(jnp.int32, (64, 128), 0)
        is_re = (row // CH) % 2 == 0
        lane_seg = lax.broadcasted_iota(jnp.int32, (8, 128), 1) // 16
        for t in range(tiles):
            lanes = slice(t * 128, t * 128 + 128)
            near = jnp.concatenate([powers[t - 1], powers[t], powers[(t + 1) % tiles]], axis=1)
            both = jnp.dot(near, smooth_ref[t], preferred_element_type=F32)
            smooth = (both[:64] + both[64:]) * (1.0 / (2 * SMOOTH + 1))
            scale = taper_ref[:, lanes] * lax.rsqrt(smooth + 1e-06)
            spec = (jnp.where(is_re, re_ref[:, lanes], im_ref[:, lanes]) * scale).astype(BF)
            spread = jnp.dot(spec, spread_ref[...], preferred_element_type=F32)
            groups = []
            for u in range(8):
                chunk = spread[:, u * 128 : u * 128 + 128]
                acc = chunk[0:8]
                for s in range(1, SEGS):
                    acc = jnp.where(lane_seg == s, chunk[s * 8 : s * 8 + 8], acc)
                groups.append(acc)
            out_ref[t * 64 : t * 64 + 64, :] = jnp.concatenate(groups, axis=0).astype(BF)


def spectra_of(pick, got):
    whole = lambda shape: pl.BlockSpec(shape, lambda i: (0,) * len(shape))
    return pl.pallas_call(
        spectra_kernel,
        grid=(8,),
        out_shape=jax.ShapeDtypeStruct((1024, 128), BF),
        in_specs=[
            whole((8, SLOTS)),
            whole((SLOTS, WIN)),
            whole((16, 384, 128)),
            whole((1, NF)),
            whole((128, 1024)),
            pl.BlockSpec((1, NT, 512), lambda i: (i, 0, 0)),
        ],
        out_specs=whole((1024, 128)),
        scratch_shapes=[
            pltpu.VMEM((64, NT), F32),
            pltpu.VMEM((64, NF), F32),
            pltpu.VMEM((64, NF), F32),
        ],
        compiler_params=pltpu.CompilerParams(vmem_limit_bytes=40 * 2**20),
        cost_estimate=pl.CostEstimate(flops=2 * 64 * NT * NT, bytes_accessed=NT * NT * 2, transcendentals=0),
        name="spectra",
    )(pick, got, smooth_table(), taper_row(), spread_table(), dft_table())


def pair_kernel(pos_ref, a_ref, b_ref, lag_ref, out_ref, x_ref, y_ref, f_ref):
    nrow, ncol = b_ref.shape[0], a_ref.shape[0]
    sub = lax.broadcasted_iota(jnp.int32, (16, 128), 0)
    lane = lax.broadcasted_iota(jnp.int32, (16, 128), 1)
    diagonal = (lane % GRP == sub).astype(F32)
    first = (lane // CH) % 2 == 0
    swap_sign = jnp.where(lax.broadcasted_iota(jnp.int32, (16, 128), 0) % 8 < 4, 1.0, -1.0)

    def group(g, special):
        rows = pl.ds(pl.multiple_of(g * 16, 16), 16)
        tiles = [a_ref[d, rows, :] for d in range(ncol)]
        turned = []
        for d in range(ncol):
            v = tiles[d].astype(F32)
            v = jnp.concatenate([pltpu.roll(v[0:8], 4, 0), pltpu.roll(v[8:16], 4, 0)], axis=0)
            turned.append(v * swap_sign)
        own = [b_ref[d, rows, :].astype(F32) for d in range(nrow)]
        prods = []
        for h in range(2):
            left = jnp.concatenate([t.astype(F32)[h * 8 : h * 8 + 8] for t in tiles], axis=0)
            right = jnp.concatenate([t[h * 8 : h * 8 + 8] for t in turned], axis=0)
            w = jnp.concatenate([left, right], axis=1).astype(BF)
            blocks = []
            for d in range(nrow):
                for c in range(CH):
                    r = h * 8 + c
                    re = own[d][r : r + 1, :] * diagonal
                    im = own[d][r + CH : r + CH + 1, :] * diagonal
                    blocks.append(jnp.concatenate([re, im], axis=1).astype(BF))
            lhs = jnp.concatenate(blocks, axis=0)
            prods.append(
                lax.dot_general(lhs, w, (((1,), (1,)), ((), ())), preferred_element_type=F32)
            )
        pairs = nrow * CH // 2
        for jp in range(pairs):
            parts = []
            for h in range(2):
                t0 = prods[h][jp * 16 : jp * 16 + 16]
                t1 = prods[h][(jp + pairs) * 16 : (jp + pairs) * 16 + 16]
                re = jnp.where(first, t0, pltpu.roll(t1, 4, 1))
                im = jnp.where(first, pltpu.roll(t0, 124, 1), t1)
                parts += [re, im]
            re0, im0, re1, im1 = parts
            sums = [re0 + re1, im0 - im1, re0 - re1, im0 + im1]
            if special:
                top = sub == 0
                sums = [
                    jnp.where(top, re0, sums[0]),
                    jnp.where(top, re1, sums[1]),
                    jnp.where(top, re0, sums[2]),
                    jnp.where(top, im1, sums[3]),
                ]
            for k in range(4):
                x_ref[k, rows, jp * 128 : jp * 128 + 128] = sums[k].astype(BF)

    group(0, True)

    @pl.loop(1, NGRP)
    def _(g):
        group(g, False)

    @pl.loop(0, 8)
    def _(n):
        cols = pl.ds(pl.multiple_of(n * 256, 256), 256)
        for odd in range(2):
            y = jnp.dot(lag_ref[2 * odd], x_ref[2 * odd, :, cols], preferred_element_type=F32)
            y += jnp.dot(lag_ref[2 * odd + 1], x_ref[2 * odd + 1, :, cols], preferred_element_type=F32)
            y_ref[0, pl.ds(odd, LAGS // 2, stride=2), :] = y[:, :128]
            y_ref[1, pl.ds(odd, LAGS // 2, stride=2), :] = y[:, 128:]
        for k in range(2):
            at = pl.ds(pl.multiple_of((n * 2 + k) * 128, 128), 128)
            for t in range(LAGS // 128):
                f_ref[t, at, :] = jnp.transpose(y_ref[k, t * 128 : t * 128 + 128, :])

    my_row, my_col = pos_ref[0], pos_ref[1]
    line = lax.broadcasted_iota(jnp.int32, (16, 128), 0)

    @pl.loop(0, ncol)
    def _(d):
        for c in range(CH):
            own = jnp.where(d == my_col, my_row * CH + c, -1)
            for e in range(2):
                drop = line + e * 16 == own
                for t in range(LAGS // 128):
                    v = f_ref[t, pl.ds(d * 8 + e * 4 + c, 16, stride=128), :]
                    v = jnp.where(drop, 0.0, v * (1.0 / math.sqrt(SEGS * NF)))
                    out_ref[d * CH + c, e * 16 : e * 16 + 16, t * 128 : t * 128 + 128] = v.astype(BF)


def pairs_of(pos, a, b):
    nrow, ncol = b.shape[0], a.shape[0]
    assert nrow * CH == 32 and ncol * CH == 64
    vmem = pl.BlockSpec(memory_space=pltpu.VMEM)
    return pl.pallas_call(
        pair_kernel,
        out_shape=jax.ShapeDtypeStruct((ncol * CH, nrow * CH, LAGS), BF),
        in_specs=[pl.BlockSpec(memory_space=pltpu.SMEM), vmem, vmem, vmem],
        out_specs=vmem,
        scratch_shapes=[
            pltpu.VMEM((4, HALF, 2048), BF),
            pltpu.VMEM((2, LAGS, 128), F32),
            pltpu.VMEM((LAGS // 128, 2048, 128), F32),
        ],
        compiler_params=pltpu.CompilerParams(vmem_limit_bytes=52 * 2**20),
        cost_estimate=pl.CostEstimate(flops=2**34, bytes_accessed=16 * 2**20, transcendentals=0),
        name="pairs",
    )(pos, a, b, lag_tables())


def local(strain, file_channels, file_counts, window_start):
    nrow, ncol = lax.axis_size("row"), lax.axis_size("col")
    my_row, my_col = lax.axis_index("row"), lax.axis_index("col")
    window = lax.dynamic_slice_in_dim(strain, window_start[0], WIN, 1)
    slot = jnp.arange(SLOTS, dtype=jnp.int32)
    live = slot < file_counts[0]
    owner = jnp.where(live, file_channels // CH // ncol, -1)
    place = file_channels % CH
    before = (owner[None, :] == owner[:, None]) & (slot[None, :] < slot[:, None])
    rank = jnp.sum(before.astype(jnp.int32), axis=1)
    lines = jnp.arange(2 * nrow, dtype=jnp.int32)
    choose = (owner[None, :] == lines[:, None] // 2) & (rank[None, :] == lines[:, None] % 2)
    labels = jnp.sum(jnp.where(choose, place[None, :] + 1, 0), axis=1) - 1
    bundle = jnp.dot(choose.astype(BF), window, preferred_element_type=F32).astype(BF)
    tags = jnp.broadcast_to(labels.astype(BF)[:, None], (2 * nrow, 128))
    sent = jnp.concatenate([bundle, tags], axis=1).reshape(nrow, 2, WIN + 128)
    got = lax.all_to_all(sent, "row", 0, 0).reshape(2 * nrow, WIN + 128)
    wanted = (jnp.arange(8, dtype=jnp.int32) % CH).astype(F32)
    pick = (got[:, WIN].astype(F32)[None, :] == wanted[:, None]).astype(BF)
    own = spectra_of(pick, got[:, :WIN])
    b = lax.all_gather(own, "row", axis=0)
    a = lax.all_gather(own, "col", axis=0)
    pos = jnp.stack([my_row, my_col]).astype(jnp.int32)
    return pairs_of(pos, a, b)


def solution(mesh):
    placed = (P(("row", "col"), None), P(("row", "col")), P(("row", "col")), P(("row", "col")))
    return jax.shard_map(
        local, mesh=mesh, in_specs=placed, out_specs=P("row", "col", None), check_vma=False
    )
```

```python
import functools
import math

import jax
import jax.numpy as jnp
import numpy as np
from jax import lax
from jax.experimental import pallas as pl
from jax.experimental.pallas import tpu as pltpu
from jax.sharding import PartitionSpec as P

NF = 2048
NT = 4096
LAGS = 1024
SEGS = 8
CH = 4
SLOTS = 16
SMOOTH = 32
EDGE = 128
WIN = SEGS * NT
HALF = NF // 2
GRP = 16
NGRP = HALF // GRP
BF = jnp.bfloat16
F32 = jnp.float32


def frequency_order():
    p = np.arange(HALF).reshape(NGRP, 1, GRP)
    mirror = np.where(p == 0, HALF, NF - p)
    return np.concatenate([p, mirror], axis=1).reshape(NF)


def trig(product, size):
    angle = (product % size).astype(np.float32) * np.float32(2.0 * math.pi / size)
    return np.cos(angle.astype(np.float64)), -np.sin(angle.astype(np.float64))


@functools.cache
def dft_table():
    order = frequency_order().astype(np.int64)
    cos, sin = trig(np.arange(NT, dtype=np.int64)[:, None] * order[None, :], NT)
    both = np.stack([cos.reshape(NT, 8, 256), sin.reshape(NT, 8, 256)], axis=2)
    return both.transpose(1, 0, 2, 3).reshape(8, NT, 512).astype(jnp.bfloat16)


@functools.cache
def smooth_table():
    order = frequency_order()
    near = np.abs(order[:, None] - order[None, :]) <= SMOOTH
    tiles = NF // 128
    out = np.zeros((tiles, 3, 128, 128), np.float32)
    for t in range(tiles):
        for k in range(3):
            s = (t + k - 1) % tiles
            out[t, k] = near[s * 128 : s * 128 + 128, t * 128 : t * 128 + 128]
    assert out.sum() == near.sum()
    return out.reshape(tiles, 384, 128).astype(jnp.bfloat16)


@functools.cache
def taper_row():
    f = frequency_order().astype(np.float64)
    rising = np.minimum(np.minimum(f + 0.5, NF - f - 0.5) / EDGE, 1.0)
    return (np.sin(0.5 * math.pi * rising) ** 2).astype(np.float32).reshape(1, NF)


@functools.cache
def spread_table():
    lane = np.arange(128)
    out = np.zeros((128, 8, 128), np.float32)
    for u in range(8):
        out[:, u] = (lane[:, None] // 16 == u) & (lane[:, None] % 16 == lane[None, :] % 16)
    return out.reshape(128, 1024).astype(jnp.bfloat16)


@functools.cache
def lag_tables():
    p = np.arange(HALF, dtype=np.int64)
    out = np.zeros((4, LAGS // 2, HALF), np.float32)
    for odd in range(2):
        m = np.arange(odd, LAGS, 2, dtype=np.int64) - LAGS // 2
        cos, sin = trig(m[:, None] * p[None, :], NT)
        mid_cos, mid_sin = trig(m * HALF, NT)
        out[2 * odd], out[2 * odd + 1] = cos, sin
        out[2 * odd + 1, :, 0] = np.rint(mid_sin if odd else mid_cos)
    return out.astype(jnp.bfloat16)


def spectra_kernel(pick_ref, got_ref, smooth_ref, taper_ref, spread_ref, table_ref, out_ref, x_ref, re_ref, im_ref):
    step = pl.program_id(0)

    @pl.when(step == 0)
    def _():
        for s in range(SEGS):
            seg = got_ref[:, s * NT : (s + 1) * NT]
            x = jnp.dot(pick_ref[...], seg, preferred_element_type=F32)
            x_ref[s * 8 : s * 8 + 8, :] = x

    prod = jnp.dot(x_ref[...].astype(BF), table_ref[0], preferred_element_type=F32)
    cols = pl.ds(pl.multiple_of(step * 256, 256), 256)
    re_ref[:, cols] = prod[:, :256]
    im_ref[:, cols] = prod[:, 256:]

    @pl.when(step == pl.num_programs(0) - 1)
    def _():
        tiles = NF // 128

        def power(t):
            lanes = slice(t % tiles * 128, t % tiles * 128 + 128)
            re, im = re_ref[:, lanes], im_ref[:, lanes]
            p = re * re + im * im
            hi = p.astype(BF)
            return jnp.concatenate([hi, (p - hi.astype(F32)).astype(BF)], axis=0)

        powers = [power(t) for t in range(tiles)]
        row = lax.broadcasted_iota(jnp.int32, (64, 128), 0)
        is_re = (row // CH) % 2 == 0
        lane_seg = lax.broadcasted_iota(jnp.int32, (8, 128), 1) // 16
        for t in range(tiles):
            lanes = slice(t * 128, t * 128 + 128)
            near = jnp.concatenate([powers[t - 1], powers[t], powers[(t + 1) % tiles]], axis=1)
            both = jnp.dot(near, smooth_ref[t], preferred_element_type=F32)
            smooth = (both[:64] + both[64:]) * (1.0 / (2 * SMOOTH + 1))
            scale = taper_ref[:, lanes] * lax.rsqrt(smooth + 1e-06)
            spec = (jnp.where(is_re, re_ref[:, lanes], im_ref[:, lanes]) * scale).astype(BF)
            spread = jnp.dot(spec, spread_ref[...], preferred_element_type=F32)
            groups = []
            for u in range(8):
                chunk = spread[:, u * 128 : u * 128 + 128]
                acc = chunk[0:8]
                for s in range(1, SEGS):
                    acc = jnp.where(lane_seg == s, chunk[s * 8 : s * 8 + 8], acc)
                groups.append(acc)
            out_ref[t * 64 : t * 64 + 64, :] = jnp.concatenate(groups, axis=0).astype(BF)


def spectra_of(pick, got):
    whole = lambda shape: pl.BlockSpec(shape, lambda i: (0,) * len(shape))
    return pl.pallas_call(
        spectra_kernel,
        grid=(8,),
        out_shape=jax.ShapeDtypeStruct((1024, 128), BF),
        in_specs=[
            whole((8, SLOTS)),
            whole((SLOTS, WIN)),
            whole((16, 384, 128)),
            whole((1, NF)),
            whole((128, 1024)),
            pl.BlockSpec((1, NT, 512), lambda i: (i, 0, 0)),
        ],
        out_specs=whole((1024, 128)),
        scratch_shapes=[
            pltpu.VMEM((64, NT), F32),
            pltpu.VMEM((64, NF), F32),
            pltpu.VMEM((64, NF), F32),
        ],
        compiler_params=pltpu.CompilerParams(vmem_limit_bytes=40 * 2**20),
        cost_estimate=pl.CostEstimate(flops=2 * 64 * NT * NT, bytes_accessed=NT * NT * 2, transcendentals=0),
        name="spectra",
    )(pick, got, smooth_table(), taper_row(), spread_table(), dft_table())


CHUNKS = 4


def pair_kernel(pos_ref, a_hbm, *refs):
    nrow, ncol = 8, 16
    b_hbm = refs[:nrow]
    lag_hbm, out_hbm, a_ref, b_ref, lag_ref, x_ref, y_ref, f_ref, o_ref, in_sem, lag_sem, out_sem = refs[nrow:]
    size = 1024 // CHUNKS

    def arrive(k):
        rows = pl.ds(k * size, size)
        copies = [pltpu.make_async_copy(a_hbm.at[:, rows, :], a_ref.at[:, rows, :], in_sem.at[k, nrow])]
        for r in range(nrow):
            copies.append(
                pltpu.make_async_copy(
                    b_hbm[r].at[rows, :], b_ref.at[pos_ref[2 + r], rows, :], in_sem.at[k, r]))
        return copies

    for k in range(CHUNKS):
        for copy in arrive(k):
            copy.start()
    lag_copy = pltpu.make_async_copy(lag_hbm, lag_ref, lag_sem)
    lag_copy.start()

    sub = lax.broadcasted_iota(jnp.int32, (16, 128), 0)
    lane = lax.broadcasted_iota(jnp.int32, (16, 128), 1)
    diagonal = (lane % GRP == sub).astype(F32).astype(BF)
    first = (lane // CH) % 2 == 0
    swap_sign = jnp.where(sub % 8 < 4, 1.0, -1.0)

    def group(g, special):
        rows = pl.ds(pl.multiple_of(g * 16, 16), 16)
        tiles = [a_ref[d, rows, :] for d in range(ncol)]
        turned = []
        for d in range(ncol):
            v = tiles[d].astype(F32)
            v = jnp.concatenate([pltpu.roll(v[0:8], 4, 0), pltpu.roll(v[8:16], 4, 0)], axis=0)
            turned.append(v * swap_sign)
        own = [b_ref[d, rows, :].astype(F32) for d in range(nrow)]
        prods = []
        for h in range(2):
            left = jnp.concatenate([t.astype(F32)[h * 8 : h * 8 + 8] for t in tiles], axis=0)
            right = jnp.concatenate([t[h * 8 : h * 8 + 8] for t in turned], axis=0)
            w = jnp.concatenate([left, right], axis=1).astype(BF)
            blocks = []
            for d in range(nrow):
                for c in range(CH):
                    r = h * 8 + c
                    re = jnp.broadcast_to(own[d][r : r + 1, :], (16, 128)).astype(BF)
                    im = jnp.broadcast_to(own[d][r + CH : r + CH + 1, :], (16, 128)).astype(BF)
                    blocks.append(jnp.concatenate([re * diagonal, im * diagonal], axis=1))
            lhs = jnp.concatenate(blocks, axis=0)
            prods.append(
                lax.dot_general(lhs, w, (((1,), (1,)), ((), ())), preferred_element_type=F32)
            )
        pairs = nrow * CH // 2
        for jp in range(pairs):
            parts = []
            for h in range(2):
                t0 = prods[h][jp * 16 : jp * 16 + 16]
                t1 = prods[h][(jp + pairs) * 16 : (jp + pairs) * 16 + 16]
                re = jnp.where(first, t0, pltpu.roll(t1, 4, 1))
                im = jnp.where(first, pltpu.roll(t0, 124, 1), t1)
                parts += [re, im]
            re0, im0, re1, im1 = parts
            sums = [re0 + re1, im0 - im1, re0 - re1, im0 + im1]
            if special:
                top = sub == 0
                sums = [
                    jnp.where(top, re0, sums[0]),
                    jnp.where(top, re1, sums[1]),
                    jnp.where(top, re0, sums[2]),
                    jnp.where(top, im1, sums[3]),
                ]
            for k in range(4):
                x_ref[k, rows, jp * 128 : jp * 128 + 128] = sums[k].astype(BF)

    @pl.loop(0, CHUNKS)
    def _(k):
        for copy in arrive(k):
            copy.wait()

        @pl.loop(0, NGRP // CHUNKS, step=4)
        def _(g):
            for u in range(4):
                group(k * (NGRP // CHUNKS) + g + u, False)

    group(0, True)
    lag_copy.wait()

    @pl.loop(0, 8)
    def _(n):
        cols = pl.ds(pl.multiple_of(n * 256, 256), 256)
        for odd in range(2):
            y = jnp.dot(lag_ref[2 * odd], x_ref[2 * odd, :, cols], preferred_element_type=F32)
            y += jnp.dot(lag_ref[2 * odd + 1], x_ref[2 * odd + 1, :, cols], preferred_element_type=F32)
            y_ref[0, pl.ds(odd, LAGS // 2, stride=2), :] = y[:, :128]
            y_ref[1, pl.ds(odd, LAGS // 2, stride=2), :] = y[:, 128:]
        for k in range(2):
            at = pl.ds((n * 2 + k) * 129, 128)
            for t in range(LAGS // 128):
                f_ref[t, at, :] = jnp.transpose(y_ref[k, t * 128 : t * 128 + 128, :])

    my_row, my_col = pos_ref[0], pos_ref[1]
    line = lax.broadcasted_iota(jnp.int32, (16, 128), 0)

    def leave(d):
        return pltpu.make_async_copy(
            o_ref.at[d % 2], out_hbm.at[pl.ds(d * CH, CH), :, :], out_sem.at[d % 2])

    @pl.loop(0, ncol)
    def _(d):
        @pl.when(d >= 2)
        def _():
            leave(d - 2).wait()

        for c in range(CH):
            own = jnp.where(d == my_col, my_row * CH + c, -1)
            for e in range(2):
                drop = line + e * 16 == own
                for t in range(LAGS // 128):
                    v = f_ref[t, pl.ds(d * 8 + e * 4 + c, 16, stride=129), :]
                    v = jnp.where(drop, 0.0, v * (1.0 / math.sqrt(SEGS * NF)))
                    o_ref[d % 2, c, e * 16 : e * 16 + 16, t * 128 : t * 128 + 128] = v.astype(BF)
        leave(d).start()

    leave(ncol - 2).wait()
    leave(ncol - 1).wait()


def pairs_of(pos, a, b):
    nrow, ncol = len(b), a.shape[0]
    assert nrow == 8 and ncol == 16
    anywhere = pl.BlockSpec(memory_space=pl.ANY)
    return pl.pallas_call(
        pair_kernel,
        out_shape=jax.ShapeDtypeStruct((ncol * CH, nrow * CH, LAGS), BF),
        in_specs=[pl.BlockSpec(memory_space=pltpu.SMEM)] + [anywhere] * (nrow + 2),
        out_specs=anywhere,
        scratch_shapes=[
            pltpu.VMEM((ncol, 1024, 128), BF),
            pltpu.VMEM((nrow, 1024, 128), BF),
            pltpu.VMEM((4, LAGS // 2, HALF), BF),
            pltpu.VMEM((4, HALF, 2048), BF),
            pltpu.VMEM((2, LAGS, 128), F32),
            pltpu.VMEM((LAGS // 128, 16 * 129 + 8, 128), F32),
            pltpu.VMEM((2, CH, nrow * CH, LAGS), BF),
            pltpu.SemaphoreType.DMA((CHUNKS, nrow + 1)),
            pltpu.SemaphoreType.DMA,
            pltpu.SemaphoreType.DMA((2,)),
        ],
        compiler_params=pltpu.CompilerParams(vmem_limit_bytes=52 * 2**20),
        cost_estimate=pl.CostEstimate(flops=2**34, bytes_accessed=16 * 2**20, transcendentals=0),
        name="pairs",
    )(pos, a, *b, lag_tables())


def over_row(own, my_row):
    def move(block, step, across=0):
        pairs = [(y * 4 + z, (y ^ across) * 4 + (z + step) % 4) for y in range(2) for z in range(4)]
        return lax.ppermute(block, "row", pairs)

    y, z = my_row // 4, my_row % 4
    index = lambda step, across: (y ^ across) * 4 + (z + step) % 4
    other = move(own, 0, 1)
    left, right = move(own, 1), move(own, -1)
    other_left, other_right = move(other, 1), move(other, -1)
    far, other_far = move(left, 1), move(other_right, -1)
    blocks = [own, other, left, right, other_left, other_right, far, other_far]
    rows = [
        index(0, 0), index(0, 1), index(-1, 0), index(1, 0),
        index(-1, 1), index(1, 1), index(2, 0), index(2, 1),
    ]
    return blocks, rows


def local(strain, file_channels, file_counts, window_start):
    nrow, ncol = lax.axis_size("row"), lax.axis_size("col")
    my_row, my_col = lax.axis_index("row"), lax.axis_index("col")
    window = lax.dynamic_slice_in_dim(strain, window_start[0], WIN, 1)
    slot = jnp.arange(SLOTS, dtype=jnp.int32)
    live = slot < file_counts[0]
    owner = jnp.where(live, file_channels // CH // ncol, -1)
    place = file_channels % CH
    before = (owner[None, :] == owner[:, None]) & (slot[None, :] < slot[:, None])
    rank = jnp.sum(before.astype(jnp.int32), axis=1)
    lines = jnp.arange(2 * nrow, dtype=jnp.int32)
    choose = (owner[None, :] == lines[:, None] // 2) & (rank[None, :] == lines[:, None] % 2)
    labels = jnp.sum(jnp.where(choose, place[None, :] + 1, 0), axis=1) - 1
    bundle = jnp.dot(choose.astype(BF), window, preferred_element_type=F32).astype(BF)
    tags = jnp.broadcast_to(labels.astype(BF)[:, None], (2 * nrow, 128))
    sent = jnp.concatenate([bundle, tags], axis=1).reshape(nrow, 2, WIN + 128)
    got = lax.all_to_all(sent, "row", 0, 0).reshape(2 * nrow, WIN + 128)
    wanted = (jnp.arange(8, dtype=jnp.int32) % CH).astype(F32)
    pick = (got[:, WIN].astype(F32)[None, :] == wanted[:, None]).astype(BF)
    own = spectra_of(pick, got[:, :WIN])
    a = lax.all_gather(own, "col", axis=0)
    b, rows = over_row(own, my_row)
    pos = jnp.stack([my_row, my_col, *rows]).astype(jnp.int32)
    return pairs_of(pos, a, b)


def solution(mesh):
    placed = (P(("row", "col"), None), P(("row", "col")), P(("row", "col")), P(("row", "col")))
    return jax.shard_map(
        local, mesh=mesh, in_specs=placed, out_specs=P("row", "col", None), check_vma=False
    )
```

```python
import functools
import math

import jax
import jax.numpy as jnp
import numpy as np
from jax import lax
from jax.experimental import pallas as pl
from jax.experimental.pallas import tpu as pltpu
from jax.sharding import PartitionSpec as P

NF = 2048
NT = 4096
LAGS = 1024
SEGS = 8
CH = 4
SLOTS = 16
SMOOTH = 32
EDGE = 128
WIN = SEGS * NT
HALF = NF // 2
GRP = 16
NGRP = HALF // GRP
BF = jnp.bfloat16
F32 = jnp.float32


def trig(product, size):
    angle = (product % size).astype(np.float32) * np.float32(2.0 * math.pi / size)
    return np.cos(angle.astype(np.float64)), -np.sin(angle.astype(np.float64))


@functools.cache
def dft_table():
    p = np.arange(HALF, dtype=np.int64)
    parts = []
    for odd in range(2):
        n = np.arange(odd, NT, 2, dtype=np.int64)
        cos, sin = trig(n[:, None] * p[None, :], NT)
        mid_cos, mid_sin = trig(n * HALF, NT)
        sin[:, 0] = np.rint(mid_sin if odd else mid_cos)
        both = np.stack([cos.reshape(NT // 2, 8, 128), sin.reshape(NT // 2, 8, 128)], axis=2)
        parts.append(both.transpose(1, 0, 2, 3).reshape(8, NT // 2, 256))
    return np.stack(parts, axis=1).astype(jnp.bfloat16)


@functools.cache
def parting_table():
    lane = np.arange(256)
    return (lane[:, None] == (lane % 128 * 2 + lane // 128)[None, :]).astype(jnp.bfloat16)


@functools.cache
def smooth_tables():
    p = np.arange(HALF)
    order = np.concatenate([p, np.where(p == 0, HALF, NF - p)]).reshape(16, 128)
    tables, use, count = [], [], 0
    for t in range(16):
        near = [np.abs(order[s][:, None] - order[t][None, :]) <= SMOOTH for s in range(16)]
        tiles = [s for s in range(16) if near[s].any()]
        table = np.zeros((4, 128, 128), np.float32)
        for k, s in enumerate(tiles):
            table[k] = near[s]
        count += table.sum()
        tiles += [t] * (4 - len(tiles))
        same = [k for k, other in enumerate(tables) if (other == table).all()]
        if not same:
            tables.append(table)
        use.append((tiles, same[0] if same else len(tables) - 1))
    f = np.arange(NF)
    assert count == (np.minimum(f + SMOOTH, NF - 1) - np.maximum(f - SMOOTH, 0) + 1).sum()
    return np.stack(tables).reshape(len(tables), 512, 128).astype(jnp.bfloat16), tuple(use)


@functools.cache
def taper_rows():
    p = np.arange(HALF)
    f = np.stack([p, np.where(p == 0, HALF, NF - p)]).astype(np.float64)
    rising = np.minimum(np.minimum(f + 0.5, NF - f - 0.5) / EDGE, 1.0)
    return (np.sin(0.5 * math.pi * rising) ** 2).astype(np.float32)


@functools.cache
def spread_table():
    lane = np.arange(128)
    out = np.zeros((128, 8, 128), np.float32)
    for u in range(8):
        out[:, u] = (lane[:, None] // 16 == u) & (lane[:, None] % 16 == lane[None, :] % 16)
    return out.reshape(128, 1024).astype(jnp.bfloat16)


@functools.cache
def lag_tables():
    p = np.arange(HALF, dtype=np.int64)
    out = np.zeros((4, LAGS // 2, HALF), np.float32)
    for odd in range(2):
        m = np.arange(odd, LAGS, 2, dtype=np.int64) - LAGS // 2
        cos, sin = trig(m[:, None] * p[None, :], NT)
        mid_cos, mid_sin = trig(m * HALF, NT)
        out[2 * odd], out[2 * odd + 1] = cos, sin
        out[2 * odd + 1, :, 0] = np.rint(mid_sin if odd else mid_cos)
    return out.astype(jnp.bfloat16)


def spectra_kernel(got_ref, part_ref, smooth_ref, taper_ref, spread_ref, table_hbm, out_ref,
                   table_ref, x_ref, half_ref, re_ref, im_ref, power_ref, sem):
    def arrive(k):
        return pltpu.make_async_copy(table_hbm.at[k], table_ref.at[k], sem.at[k])

    for k in range(8):
        arrive(k).start()
    tags = jnp.transpose(got_ref[:, WIN : WIN + 128].astype(F32))[0:8]
    wanted = lax.broadcasted_iota(jnp.int32, (8, SLOTS), 0) % CH
    pick = (tags == wanted.astype(F32)).astype(F32).astype(BF)
    for s in range(SEGS):
        seg = got_ref[:, s * NT : (s + 1) * NT]
        x_ref[s * 8 : s * 8 + 8, :] = jnp.dot(pick, seg, preferred_element_type=F32)
    for t in range(NT // 256):
        x = x_ref[:, t * 256 : t * 256 + 256].astype(BF)
        parted = jnp.dot(x, part_ref[...], preferred_element_type=F32).astype(BF)
        half_ref[0, :, t * 128 : t * 128 + 128] = parted[:, :128]
        half_ref[1, :, t * 128 : t * 128 + 128] = parted[:, 128:]

    lane0 = lax.broadcasted_iota(jnp.int32, (64, 128), 1) == 0

    @pl.loop(0, 8)
    def _(k):
        arrive(k).wait()
        even = jnp.dot(half_ref[0], table_ref[k, 0], preferred_element_type=F32)
        odd = jnp.dot(half_ref[1], table_ref[k, 1], preferred_element_type=F32)
        ec, es, oc, os = even[:, :128], even[:, 128:], odd[:, :128], odd[:, 128:]
        middle = lane0 & (k == 0)
        re = [ec + oc, jnp.where(middle, es, ec - oc)]
        im = [jnp.where(middle, 0.0, es + os), jnp.where(middle, os, os - es)]
        for h in range(2):
            re_ref[h, k] = re[h]
            im_ref[h, k] = im[h]
            power = re[h] * re[h] + im[h] * im[h]
            hi = power.astype(BF)
            power_ref[h, k, 0:64, :] = hi
            power_ref[h, k, 64:128, :] = (power - hi.astype(F32)).astype(BF)

    use = smooth_tables()[1]
    is_re = (lax.broadcasted_iota(jnp.int32, (64, 128), 0) // CH) % 2 == 0
    lane_seg = lax.broadcasted_iota(jnp.int32, (8, 128), 1) // 16
    for t in range(8):
        halves = []
        for h in range(2):
            tiles, number = use[h * 8 + t]
            near = jnp.concatenate([power_ref[k // 8, k % 8] for k in tiles], axis=1)
            both = jnp.dot(near, smooth_ref[number], preferred_element_type=F32)
            smooth = (both[:64] + both[64:]) * (1.0 / (2 * SMOOTH + 1))
            scale = taper_ref[h : h + 1, t * 128 : t * 128 + 128] * lax.rsqrt(smooth + 1e-06)
            spec = (jnp.where(is_re, re_ref[h, t], im_ref[h, t]) * scale).astype(BF)
            spread = jnp.dot(spec, spread_ref[...], preferred_element_type=F32)
            chunks = []
            for u in range(8):
                chunk = spread[:, u * 128 : u * 128 + 128]
                acc = chunk[0:8]
                for s in range(1, SEGS):
                    acc = jnp.where(lane_seg == s, chunk[s * 8 : s * 8 + 8], acc)
                chunks.append(acc)
            halves.append(chunks)
        for u in range(8):
            rows = jnp.concatenate([halves[0][u], halves[1][u]], axis=0).astype(BF)
            out_ref[(t * 8 + u) * 16 : (t * 8 + u) * 16 + 16, :] = rows


def spectra_of(got):
    vmem = pl.BlockSpec(memory_space=pltpu.VMEM)
    return pl.pallas_call(
        spectra_kernel,
        out_shape=jax.ShapeDtypeStruct((1024, 128), BF),
        in_specs=[vmem] * 5 + [pl.BlockSpec(memory_space=pl.ANY)],
        out_specs=vmem,
        scratch_shapes=[
            pltpu.VMEM((8, 2, NT // 2, 256), BF),
            pltpu.VMEM((64, NT), F32),
            pltpu.VMEM((2, 64, NT // 2), BF),
            pltpu.VMEM((2, 8, 64, 128), F32),
            pltpu.VMEM((2, 8, 64, 128), F32),
            pltpu.VMEM((2, 8, 128, 128), BF),
            pltpu.SemaphoreType.DMA((8,)),
        ],
        compiler_params=pltpu.CompilerParams(vmem_limit_bytes=40 * 2**20),
        cost_estimate=pl.CostEstimate(flops=2**31, bytes_accessed=NT * NT, transcendentals=0),
        name="spectra",
    )(got, parting_table(), smooth_tables()[0], taper_rows(), spread_table(), dft_table())


CHUNKS = 4


def pair_kernel(pos_ref, a_hbm, *refs):
    nrow, ncol = 8, 16
    b_hbm = refs[:nrow]
    lag_hbm, out_hbm, a_ref, b_ref, lag_ref, x_ref, y_ref, f_ref, o_ref, in_sem, lag_sem, out_sem = refs[nrow:]
    size = 1024 // CHUNKS

    def arrive(k):
        rows = pl.ds(k * size, size)
        copies = [pltpu.make_async_copy(a_hbm.at[:, rows, :], a_ref.at[:, rows, :], in_sem.at[k, nrow])]
        for r in range(nrow):
            copies.append(
                pltpu.make_async_copy(
                    b_hbm[r].at[rows, :], b_ref.at[pos_ref[2 + r], rows, :], in_sem.at[k, r]))
        return copies

    for k in range(CHUNKS):
        for copy in arrive(k):
            copy.start()
    lag_copy = pltpu.make_async_copy(lag_hbm, lag_ref, lag_sem)
    lag_copy.start()

    sub = lax.broadcasted_iota(jnp.int32, (16, 128), 0)
    lane = lax.broadcasted_iota(jnp.int32, (16, 128), 1)
    diagonal = (lane % GRP == sub).astype(F32).astype(BF)
    first = (lane // CH) % 2 == 0
    swap_sign = jnp.where(sub % 8 < 4, 1.0, -1.0)

    def group(g, special):
        rows = pl.ds(pl.multiple_of(g * 16, 16), 16)
        tiles = [a_ref[d, rows, :] for d in range(ncol)]
        turned = []
        for d in range(ncol):
            v = tiles[d].astype(F32)
            v = jnp.concatenate([pltpu.roll(v[0:8], 4, 0), pltpu.roll(v[8:16], 4, 0)], axis=0)
            turned.append(v * swap_sign)
        own = [b_ref[d, rows, :].astype(F32) for d in range(nrow)]
        prods = []
        for h in range(2):
            left = jnp.concatenate([t.astype(F32)[h * 8 : h * 8 + 8] for t in tiles], axis=0)
            right = jnp.concatenate([t[h * 8 : h * 8 + 8] for t in turned], axis=0)
            w = jnp.concatenate([left, right], axis=1).astype(BF)
            blocks = []
            for d in range(nrow):
                for c in range(CH):
                    r = h * 8 + c
                    re = jnp.broadcast_to(own[d][r : r + 1, :], (16, 128)).astype(BF)
                    im = jnp.broadcast_to(own[d][r + CH : r + CH + 1, :], (16, 128)).astype(BF)
                    blocks.append(jnp.concatenate([re * diagonal, im * diagonal], axis=1))
            lhs = jnp.concatenate(blocks, axis=0)
            prods.append(
                lax.dot_general(lhs, w, (((1,), (1,)), ((), ())), preferred_element_type=F32)
            )
        pairs = nrow * CH // 2
        for jp in range(pairs):
            parts = []
            for h in range(2):
                t0 = prods[h][jp * 16 : jp * 16 + 16]
                t1 = prods[h][(jp + pairs) * 16 : (jp + pairs) * 16 + 16]
                re = jnp.where(first, t0, pltpu.roll(t1, 4, 1))
                im = jnp.where(first, pltpu.roll(t0, 124, 1), t1)
                parts += [re, im]
            re0, im0, re1, im1 = parts
            sums = [re0 + re1, im0 - im1, re0 - re1, im0 + im1]
            if special:
                top = sub == 0
                sums = [
                    jnp.where(top, re0, sums[0]),
                    jnp.where(top, re1, sums[1]),
                    jnp.where(top, re0, sums[2]),
                    jnp.where(top, im1, sums[3]),
                ]
            for k in range(4):
                x_ref[k, rows, jp * 128 : jp * 128 + 128] = sums[k].astype(BF)

    @pl.loop(0, CHUNKS)
    def _(k):
        for copy in arrive(k):
            copy.wait()

        @pl.loop(0, NGRP // CHUNKS, step=4)
        def _(g):
            for u in range(4):
                group(k * (NGRP // CHUNKS) + g + u, False)

    group(0, True)
    lag_copy.wait()

    @pl.loop(0, 8)
    def _(n):
        cols = pl.ds(pl.multiple_of(n * 256, 256), 256)
        for odd in range(2):
            y = jnp.dot(lag_ref[2 * odd], x_ref[2 * odd, :, cols], preferred_element_type=F32)
            y += jnp.dot(lag_ref[2 * odd + 1], x_ref[2 * odd + 1, :, cols], preferred_element_type=F32)
            y_ref[0, pl.ds(odd, LAGS // 2, stride=2), :] = y[:, :128]
            y_ref[1, pl.ds(odd, LAGS // 2, stride=2), :] = y[:, 128:]
        for k in range(2):
            at = pl.ds((n * 2 + k) * 129, 128)
            for t in range(LAGS // 128):
                f_ref[t, at, :] = jnp.transpose(y_ref[k, t * 128 : t * 128 + 128, :])

    my_row, my_col = pos_ref[0], pos_ref[1]
    line = lax.broadcasted_iota(jnp.int32, (16, 128), 0)

    def leave(d):
        return pltpu.make_async_copy(
            o_ref.at[d % 2], out_hbm.at[pl.ds(d * CH, CH), :, :], out_sem.at[d % 2])

    @pl.loop(0, ncol)
    def _(d):
        @pl.when(d >= 2)
        def _():
            leave(d - 2).wait()

        for c in range(CH):
            own = jnp.where(d == my_col, my_row * CH + c, -1)
            for e in range(2):
                drop = line + e * 16 == own
                for t in range(LAGS // 128):
                    v = f_ref[t, pl.ds(d * 8 + e * 4 + c, 16, stride=129), :]
                    v = jnp.where(drop, 0.0, v * (1.0 / math.sqrt(SEGS * NF)))
                    o_ref[d % 2, c, e * 16 : e * 16 + 16, t * 128 : t * 128 + 128] = v.astype(BF)
        leave(d).start()

    leave(ncol - 2).wait()
    leave(ncol - 1).wait()


def pairs_of(pos, a, b):
    nrow, ncol = len(b), a.shape[0]
    assert nrow == 8 and ncol == 16
    anywhere = pl.BlockSpec(memory_space=pl.ANY)
    return pl.pallas_call(
        pair_kernel,
        out_shape=jax.ShapeDtypeStruct((ncol * CH, nrow * CH, LAGS), BF),
        in_specs=[pl.BlockSpec(memory_space=pltpu.SMEM)] + [anywhere] * (nrow + 2),
        out_specs=anywhere,
        scratch_shapes=[
            pltpu.VMEM((ncol, 1024, 128), BF),
            pltpu.VMEM((nrow, 1024, 128), BF),
            pltpu.VMEM((4, LAGS // 2, HALF), BF),
            pltpu.VMEM((4, HALF, 2048), BF),
            pltpu.VMEM((2, LAGS, 128), F32),
            pltpu.VMEM((LAGS // 128, 16 * 129 + 8, 128), F32),
            pltpu.VMEM((2, CH, nrow * CH, LAGS), BF),
            pltpu.SemaphoreType.DMA((CHUNKS, nrow + 1)),
            pltpu.SemaphoreType.DMA,
            pltpu.SemaphoreType.DMA((2,)),
        ],
        compiler_params=pltpu.CompilerParams(vmem_limit_bytes=52 * 2**20),
        cost_estimate=pl.CostEstimate(flops=2**34, bytes_accessed=16 * 2**20, transcendentals=0),
        name="pairs",
    )(pos, a, *b, lag_tables())


def over_row(own, my_row):
    def move(block, step, across=0):
        pairs = [(y * 4 + z, (y ^ across) * 4 + (z + step) % 4) for y in range(2) for z in range(4)]
        return lax.ppermute(block, "row", pairs)

    y, z = my_row // 4, my_row % 4
    index = lambda step, across: (y ^ across) * 4 + (z + step) % 4
    other = move(own, 0, 1)
    left, right = move(own, 1), move(own, -1)
    other_left, other_right = move(other, 1), move(other, -1)
    far, other_far = move(left, 1), move(other_right, -1)
    blocks = [own, other, left, right, other_left, other_right, far, other_far]
    rows = [
        index(0, 0), index(0, 1), index(-1, 0), index(1, 0),
        index(-1, 1), index(1, 1), index(2, 0), index(2, 1),
    ]
    return blocks, rows


def local(strain, file_channels, file_counts, window_start):
    nrow, ncol = lax.axis_size("row"), lax.axis_size("col")
    my_row, my_col = lax.axis_index("row"), lax.axis_index("col")
    window = lax.dynamic_slice_in_dim(strain, window_start[0], WIN, 1)
    slot = jnp.arange(SLOTS, dtype=jnp.int32)
    live = slot < file_counts[0]
    owner = jnp.where(live, file_channels // CH // ncol, -1)
    place = file_channels % CH
    before = (owner[None, :] == owner[:, None]) & (slot[None, :] < slot[:, None])
    rank = jnp.sum(before.astype(jnp.int32), axis=1)
    lines = jnp.arange(2 * nrow, dtype=jnp.int32)
    choose = (owner[None, :] == lines[:, None] // 2) & (rank[None, :] == lines[:, None] % 2)
    labels = jnp.sum(jnp.where(choose, place[None, :] + 1, 0), axis=1) - 1
    bundle = jnp.dot(choose.astype(BF), window, preferred_element_type=F32).astype(BF)
    tags = jnp.broadcast_to(labels.astype(BF)[:, None], (2 * nrow, 128))
    sent = jnp.concatenate([bundle, tags], axis=1).reshape(nrow, 2, WIN + 128)
    got = lax.all_to_all(sent, "row", 0, 0).reshape(2 * nrow, WIN + 128)
    own = spectra_of(got)
    a = lax.all_gather(own, "col", axis=0)
    b, rows = over_row(own, my_row)
    pos = jnp.stack([my_row, my_col, *rows]).astype(jnp.int32)
    return pairs_of(pos, a, b)


def solution(mesh):
    placed = (P(("row", "col"), None), P(("row", "col")), P(("row", "col")), P(("row", "col")))
    return jax.shard_map(
        local, mesh=mesh, in_specs=placed, out_specs=P("row", "col", None), check_vma=False
    )
```

```python
import functools
import math

import jax
import jax.numpy as jnp
import numpy as np
from jax import lax
from jax.experimental import pallas as pl
from jax.experimental.pallas import tpu as pltpu
from jax.sharding import PartitionSpec as P

NF = 2048
NT = 4096
LAGS = 1024
SEGS = 8
CH = 4
SLOTS = 16
SMOOTH = 32
EDGE = 128
WIN = SEGS * NT
HALF = NF // 2
GRP = 16
NGRP = HALF // GRP
BF = jnp.bfloat16
F32 = jnp.float32


def trig(product, size):
    angle = (product % size).astype(np.float32) * np.float32(2.0 * math.pi / size)
    return np.cos(angle.astype(np.float64)), -np.sin(angle.astype(np.float64))


@functools.cache
def dft_table():
    p = np.arange(HALF, dtype=np.int64)
    parts = []
    for odd in range(2):
        n = np.arange(odd, NT, 2, dtype=np.int64)
        cos, sin = trig(n[:, None] * p[None, :], NT)
        mid_cos, mid_sin = trig(n * HALF, NT)
        sin[:, 0] = np.rint(mid_sin if odd else mid_cos)
        both = np.stack([cos.reshape(NT // 2, 8, 128), sin.reshape(NT // 2, 8, 128)], axis=2)
        parts.append(both.transpose(1, 0, 2, 3).reshape(8, NT // 2, 256))
    return np.stack(parts, axis=1).astype(jnp.bfloat16)


@functools.cache
def parting_table():
    lane = np.arange(256)
    return (lane[:, None] == (lane % 128 * 2 + lane // 128)[None, :]).astype(jnp.bfloat16)


@functools.cache
def smooth_tables():
    p = np.arange(HALF)
    order = np.concatenate([p, np.where(p == 0, HALF, NF - p)]).reshape(16, 128)
    tables, use, count = [], [], 0
    for t in range(16):
        near = [np.abs(order[s][:, None] - order[t][None, :]) <= SMOOTH for s in range(16)]
        tiles = [s for s in range(16) if near[s].any()]
        table = np.zeros((4, 128, 128), np.float32)
        for k, s in enumerate(tiles):
            table[k] = near[s]
        count += table.sum()
        tiles += [t] * (4 - len(tiles))
        same = [k for k, other in enumerate(tables) if (other == table).all()]
        if not same:
            tables.append(table)
        use.append((tiles, same[0] if same else len(tables) - 1))
    f = np.arange(NF)
    assert count == (np.minimum(f + SMOOTH, NF - 1) - np.maximum(f - SMOOTH, 0) + 1).sum()
    return np.stack(tables).reshape(len(tables), 512, 128).astype(jnp.bfloat16), tuple(use)


@functools.cache
def taper_rows():
    p = np.arange(HALF)
    f = np.stack([p, np.where(p == 0, HALF, NF - p)]).astype(np.float64)
    rising = np.minimum(np.minimum(f + 0.5, NF - f - 0.5) / EDGE, 1.0)
    return (np.sin(0.5 * math.pi * rising) ** 2).astype(np.float32)


@functools.cache
def spread_table():
    lane = np.arange(128)
    out = np.zeros((128, 8, 128), np.float32)
    for u in range(8):
        out[:, u] = (lane[:, None] // 16 == u) & (lane[:, None] % 16 == lane[None, :] % 16)
    return out.reshape(128, 1024).astype(jnp.bfloat16)


LAG_ROWS = 272


@functools.cache
def lag_tables():
    p = np.arange(HALF, dtype=np.int64)
    out = np.zeros((4, LAG_ROWS, HALF), np.float32)
    for odd in range(2):
        m = np.arange(odd, LAGS // 2 + 1, 2, dtype=np.int64)
        cos, sin = trig(m[:, None] * p[None, :], NT)
        out[2 * odd, : len(m)], out[2 * odd + 1, : len(m)] = cos, sin
        if odd:
            out[3, : len(m), 0] = np.rint(trig(m * HALF, NT)[1])
    return out.astype(jnp.bfloat16)


@functools.cache
def turning_tables():
    r = np.arange(256)
    return np.stack([(r[:, None] + r[None, :] == n) for n in (256, 255)]).astype(jnp.bfloat16)


def spectra_kernel(got_ref, part_ref, smooth_ref, taper_ref, spread_ref, table_hbm, out_ref,
                   table_ref, x_ref, half_ref, re_ref, im_ref, power_ref, sem):
    def arrive(k):
        return pltpu.make_async_copy(table_hbm.at[k], table_ref.at[k], sem.at[k])

    for k in range(8):
        arrive(k).start()
    tags = jnp.transpose(got_ref[:, WIN : WIN + 128].astype(F32))[0:8]
    wanted = lax.broadcasted_iota(jnp.int32, (8, SLOTS), 0) % CH
    pick = (tags == wanted.astype(F32)).astype(F32).astype(BF)
    for s in range(SEGS):
        seg = got_ref[:, s * NT : (s + 1) * NT]
        x_ref[s * 8 : s * 8 + 8, :] = jnp.dot(pick, seg, preferred_element_type=F32)
    for t in range(NT // 256):
        x = x_ref[:, t * 256 : t * 256 + 256].astype(BF)
        parted = jnp.dot(x, part_ref[...], preferred_element_type=F32).astype(BF)
        half_ref[0, :, t * 128 : t * 128 + 128] = parted[:, :128]
        half_ref[1, :, t * 128 : t * 128 + 128] = parted[:, 128:]

    lane0 = lax.broadcasted_iota(jnp.int32, (64, 128), 1) == 0

    @pl.loop(0, 8)
    def _(k):
        arrive(k).wait()
        even = jnp.dot(half_ref[0], table_ref[k, 0], preferred_element_type=F32)
        odd = jnp.dot(half_ref[1], table_ref[k, 1], preferred_element_type=F32)
        ec, es, oc, os = even[:, :128], even[:, 128:], odd[:, :128], odd[:, 128:]
        middle = lane0 & (k == 0)
        re = [ec + oc, jnp.where(middle, es, ec - oc)]
        im = [jnp.where(middle, 0.0, es + os), jnp.where(middle, os, os - es)]
        for h in range(2):
            re_ref[h, k] = re[h]
            im_ref[h, k] = im[h]
            power = re[h] * re[h] + im[h] * im[h]
            hi = power.astype(BF)
            power_ref[h, k, 0:64, :] = hi
            power_ref[h, k, 64:128, :] = (power - hi.astype(F32)).astype(BF)

    use = smooth_tables()[1]
    is_re = (lax.broadcasted_iota(jnp.int32, (64, 128), 0) // CH) % 2 == 0
    lane_seg = lax.broadcasted_iota(jnp.int32, (8, 128), 1) // 16
    for t in range(8):
        halves = []
        for h in range(2):
            tiles, number = use[h * 8 + t]
            near = jnp.concatenate([power_ref[k // 8, k % 8] for k in tiles], axis=1)
            both = jnp.dot(near, smooth_ref[number], preferred_element_type=F32)
            smooth = (both[:64] + both[64:]) * (1.0 / (2 * SMOOTH + 1))
            scale = taper_ref[h : h + 1, t * 128 : t * 128 + 128] * lax.rsqrt(smooth + 1e-06)
            spec = (jnp.where(is_re, re_ref[h, t], im_ref[h, t]) * scale).astype(BF)
            spread = jnp.dot(spec, spread_ref[...], preferred_element_type=F32)
            chunks = []
            for u in range(8):
                chunk = spread[:, u * 128 : u * 128 + 128]
                acc = chunk[0:8]
                for s in range(1, SEGS):
                    acc = jnp.where(lane_seg == s, chunk[s * 8 : s * 8 + 8], acc)
                chunks.append(acc)
            halves.append(chunks)
        for u in range(8):
            rows = jnp.concatenate([halves[0][u], halves[1][u]], axis=0).astype(BF)
            out_ref[(t * 8 + u) * 16 : (t * 8 + u) * 16 + 16, :] = rows


def spectra_of(got):
    vmem = pl.BlockSpec(memory_space=pltpu.VMEM)
    return pl.pallas_call(
        spectra_kernel,
        out_shape=jax.ShapeDtypeStruct((1024, 128), BF),
        in_specs=[vmem] * 5 + [pl.BlockSpec(memory_space=pl.ANY)],
        out_specs=vmem,
        scratch_shapes=[
            pltpu.VMEM((8, 2, NT // 2, 256), BF),
            pltpu.VMEM((64, NT), F32),
            pltpu.VMEM((2, 64, NT // 2), BF),
            pltpu.VMEM((2, 8, 64, 128), F32),
            pltpu.VMEM((2, 8, 64, 128), F32),
            pltpu.VMEM((2, 8, 128, 128), BF),
            pltpu.SemaphoreType.DMA((8,)),
        ],
        compiler_params=pltpu.CompilerParams(vmem_limit_bytes=40 * 2**20),
        cost_estimate=pl.CostEstimate(flops=2**31, bytes_accessed=NT * NT, transcendentals=0),
        name="spectra",
    )(got, parting_table(), smooth_tables()[0], taper_rows(), spread_table(), dft_table())


CHUNKS = 4


def pair_kernel(pos_ref, a_hbm, *refs):
    nrow, ncol = 8, 16
    b_hbm = refs[:nrow]
    lag_hbm, turn_ref, out_hbm, a_ref, b_ref, lag_ref, x_ref, y_ref, f_ref, o_ref, in_sem, lag_sem, out_sem = refs[nrow:]
    size = 1024 // CHUNKS

    def arrive(k):
        rows = pl.ds(k * size, size)
        copies = [pltpu.make_async_copy(a_hbm.at[:, rows, :], a_ref.at[:, rows, :], in_sem.at[k, nrow])]
        for r in range(nrow):
            copies.append(
                pltpu.make_async_copy(
                    b_hbm[r].at[rows, :], b_ref.at[pos_ref[2 + r], rows, :], in_sem.at[k, r]))
        return copies

    for k in range(CHUNKS):
        for copy in arrive(k):
            copy.start()
    lag_copy = pltpu.make_async_copy(lag_hbm, lag_ref, lag_sem)
    lag_copy.start()

    sub = lax.broadcasted_iota(jnp.int32, (16, 128), 0)
    lane = lax.broadcasted_iota(jnp.int32, (16, 128), 1)
    diagonal = (lane % GRP == sub).astype(F32).astype(BF)
    first = (lane // CH) % 2 == 0
    swap_sign = jnp.where(sub % 8 < 4, 1.0, -1.0)

    def group(g, special):
        rows = pl.ds(pl.multiple_of(g * 16, 16), 16)
        tiles = [a_ref[d, rows, :] for d in range(ncol)]
        turned = []
        for d in range(ncol):
            v = tiles[d].astype(F32)
            v = jnp.concatenate([pltpu.roll(v[0:8], 4, 0), pltpu.roll(v[8:16], 4, 0)], axis=0)
            turned.append(v * swap_sign)
        own = [b_ref[d, rows, :].astype(F32) for d in range(nrow)]
        prods = []
        for h in range(2):
            left = jnp.concatenate([t.astype(F32)[h * 8 : h * 8 + 8] for t in tiles], axis=0)
            right = jnp.concatenate([t[h * 8 : h * 8 + 8] for t in turned], axis=0)
            w = jnp.concatenate([left, right], axis=1).astype(BF)
            blocks = []
            for d in range(nrow):
                for c in range(CH):
                    r = h * 8 + c
                    re = jnp.broadcast_to(own[d][r : r + 1, :], (16, 128)).astype(BF)
                    im = jnp.broadcast_to(own[d][r + CH : r + CH + 1, :], (16, 128)).astype(BF)
                    blocks.append(jnp.concatenate([re * diagonal, im * diagonal], axis=1))
            lhs = jnp.concatenate(blocks, axis=0)
            prods.append(
                lax.dot_general(lhs, w, (((1,), (1,)), ((), ())), preferred_element_type=F32)
            )
        pairs = nrow * CH // 2
        for jp in range(pairs):
            parts = []
            for h in range(2):
                j = jp // 8 * 16 + jp % 8
                t0 = prods[h][j * 16 : j * 16 + 16]
                t1 = prods[h][(j + 8) * 16 : (j + 8) * 16 + 16]
                re = jnp.where(first, t0, pltpu.roll(t1, 4, 1))
                im = jnp.where(first, pltpu.roll(t0, 124, 1), t1)
                parts += [re, im]
            re0, im0, re1, im1 = parts
            sums = [re0 + re1, im0 - im1, re0 - re1, im0 + im1]
            if special:
                top = sub == 0
                sums = [
                    jnp.where(top, re0, sums[0]),
                    jnp.where(top, re1, sums[1]),
                    jnp.where(top, re0, sums[2]),
                    jnp.where(top, im1, sums[3]),
                ]
            for k in range(4):
                x_ref[k, rows, jp * 128 : jp * 128 + 128] = sums[k].astype(BF)

    @pl.loop(0, CHUNKS)
    def _(k):
        for copy in arrive(k):
            copy.wait()

        for u in range(NGRP // CHUNKS):
            group(k * (NGRP // CHUNKS) + u, False)

    group(0, True)
    lag_copy.wait()

    my_row, my_col = pos_ref[0], pos_ref[1]
    line = lax.broadcasted_iota(jnp.int32, (16, 128), 0)
    place = lax.broadcasted_iota(jnp.int32, (LAG_ROWS, 1), 0)
    alternate = jnp.where(place % 2 == 0, 1.0, -1.0)

    def leave(half, d):
        lines = pl.ds(half * 16, 16)
        return pltpu.make_async_copy(
            o_ref.at[pl.ds(d * CH, CH), lines, :], out_hbm.at[pl.ds(d * CH, CH), lines, :], out_sem.at[half, d])

    for half in range(2):

        @pl.loop(0, 4, unroll=4)
        def _(n):
            cols = pl.ds(pl.multiple_of(half * 1024 + n * 256, 256), 256)
            for odd in range(2):
                size = 256 if odd else LAG_ROWS
                cos = jnp.dot(lag_ref[2 * odd, :size], x_ref[2 * odd, :, cols], preferred_element_type=F32)
                sin = jnp.dot(lag_ref[2 * odd + 1, :size], x_ref[2 * odd + 1, :, cols], preferred_element_type=F32)
                if not odd:
                    cos += alternate * x_ref[1, 0:16, cols].astype(F32)[0:1]
                later = (cos + sin)[:256]
                sooner = cos - sin
                turned = jnp.dot(turn_ref[odd], sooner[:256].astype(BF), preferred_element_type=F32)
                for k in range(2):
                    half_cols = slice(k * 128, k * 128 + 128)
                    y_ref[k, pl.ds(odd, 256, stride=2), :] = turned[:, half_cols]
                    y_ref[k, pl.ds(LAGS // 2 + odd, 256, stride=2), :] = later[:, half_cols]
                    if not odd:
                        y_ref[k, 0:1, :] = sooner[256:257, half_cols]
            for k in range(2):
                at = pl.ds((n * 2 + k) * 129, 128)
                for t in range(LAGS // 128):
                    f_ref[t, at, :] = jnp.transpose(y_ref[k, t * 128 : t * 128 + 128, :])

        @pl.loop(0, ncol)
        def _(d):
            for c in range(CH):
                own = jnp.where(d == my_col, my_row * CH + c, -1)
                drop = line + half * 16 == own
                for t in range(LAGS // 128):
                    v = jnp.concatenate(
                        [f_ref[t, pl.ds(d * 8 + e * 4 + c, 8, stride=129), :] for e in range(2)], axis=0)
                    v = jnp.where(drop, 0.0, v * (1.0 / math.sqrt(SEGS * NF)))
                    o_ref[d * CH + c, half * 16 : half * 16 + 16, t * 128 : t * 128 + 128] = v.astype(BF)
            leave(half, d).start()

    for half in range(2):
        for d in range(ncol):
            leave(half, d).wait()


def pairs_of(pos, a, b):
    nrow, ncol = len(b), a.shape[0]
    assert nrow == 8 and ncol == 16
    anywhere = pl.BlockSpec(memory_space=pl.ANY)
    return pl.pallas_call(
        pair_kernel,
        out_shape=jax.ShapeDtypeStruct((ncol * CH, nrow * CH, LAGS), BF),
        in_specs=[pl.BlockSpec(memory_space=pltpu.SMEM)] + [anywhere] * (nrow + 2)
        + [pl.BlockSpec(memory_space=pltpu.VMEM)],
        out_specs=anywhere,
        scratch_shapes=[
            pltpu.VMEM((ncol, 1024, 128), BF),
            pltpu.VMEM((nrow, 1024, 128), BF),
            pltpu.VMEM((4, LAG_ROWS, HALF), BF),
            pltpu.VMEM((4, HALF, 2048), BF),
            pltpu.VMEM((2, LAGS, 128), F32),
            pltpu.VMEM((LAGS // 128, 8 * 129 + 8, 128), F32),
            pltpu.VMEM((ncol * CH, nrow * CH, LAGS), BF),
            pltpu.SemaphoreType.DMA((CHUNKS, nrow + 1)),
            pltpu.SemaphoreType.DMA,
            pltpu.SemaphoreType.DMA((2, ncol)),
        ],
        compiler_params=pltpu.CompilerParams(vmem_limit_bytes=52 * 2**20),
        cost_estimate=pl.CostEstimate(flops=2**34, bytes_accessed=16 * 2**20, transcendentals=0),
        name="pairs",
    )(pos, a, *b, lag_tables(), turning_tables())


def over_row(own, my_row):
    def move(block, step, across=0):
        pairs = [(y * 4 + z, (y ^ across) * 4 + (z + step) % 4) for y in range(2) for z in range(4)]
        return lax.ppermute(block, "row", pairs)

    y, z = my_row // 4, my_row % 4
    index = lambda step, across: (y ^ across) * 4 + (z + step) % 4
    other = move(own, 0, 1)
    left, right = move(own, 1), move(own, -1)
    other_left, other_right = move(other, 1), move(other, -1)
    far, other_far = move(left, 1), move(other_right, -1)
    blocks = [own, other, left, right, other_left, other_right, far, other_far]
    rows = [
        index(0, 0), index(0, 1), index(-1, 0), index(1, 0),
        index(-1, 1), index(1, 1), index(2, 0), index(2, 1),
    ]
    return blocks, rows


def local(strain, file_channels, file_counts, window_start):
    nrow, ncol = lax.axis_size("row"), lax.axis_size("col")
    my_row, my_col = lax.axis_index("row"), lax.axis_index("col")
    window = lax.dynamic_slice_in_dim(strain, window_start[0], WIN, 1)
    slot = jnp.arange(SLOTS, dtype=jnp.int32)
    live = slot < file_counts[0]
    owner = jnp.where(live, file_channels // CH // ncol, -1)
    place = file_channels % CH
    before = (owner[None, :] == owner[:, None]) & (slot[None, :] < slot[:, None])
    rank = jnp.sum(before.astype(jnp.int32), axis=1)
    lines = jnp.arange(2 * nrow, dtype=jnp.int32)
    choose = (owner[None, :] == lines[:, None] // 2) & (rank[None, :] == lines[:, None] % 2)
    labels = jnp.sum(jnp.where(choose, place[None, :] + 1, 0), axis=1) - 1
    bundle = jnp.dot(choose.astype(BF), window, preferred_element_type=F32).astype(BF)
    tags = jnp.broadcast_to(labels.astype(BF)[:, None], (2 * nrow, 128))
    sent = jnp.concatenate([bundle, tags], axis=1).reshape(nrow, 2, WIN + 128)
    got = lax.all_to_all(sent, "row", 0, 0).reshape(2 * nrow, WIN + 128)
    own = spectra_of(got)
    a = lax.all_gather(own, "col", axis=0)
    b, rows = over_row(own, my_row)
    pos = jnp.stack([my_row, my_col, *rows]).astype(jnp.int32)
    return pairs_of(pos, a, b)


def solution(mesh):
    placed = (P(("row", "col"), None), P(("row", "col")), P(("row", "col")), P(("row", "col")))
    return jax.shard_map(
        local, mesh=mesh, in_specs=placed, out_specs=P("row", "col", None), check_vma=False
    )
```

```python
import functools
import math

import jax
import jax.numpy as jnp
import numpy as np
from jax import lax
from jax.experimental import pallas as pl
from jax.experimental.pallas import tpu as pltpu
from jax.sharding import PartitionSpec as P

NF = 2048
NT = 4096
LAGS = 1024
SEGS = 8
CH = 4
SLOTS = 16
SMOOTH = 32
EDGE = 128
WIN = SEGS * NT
HALF = NF // 2
QUARTER = NF // 4
GRP = 16
NGRP = HALF // GRP
BF = jnp.bfloat16
F32 = jnp.float32


def band_places():
    p = np.arange(QUARTER, dtype=np.int64)
    return np.concatenate([p, np.where(p == 0, QUARTER, HALF - p)])


def band_mirrors():
    f = band_places()
    return np.where(f == 0, HALF, NF - f)


def trig(product, size):
    angle = (product % size).astype(np.float32) * np.float32(2.0 * math.pi / size)
    return np.cos(angle.astype(np.float64)), -np.sin(angle.astype(np.float64))


@functools.cache
def dft_table():
    p = np.arange(QUARTER, dtype=np.int64)
    parts = []
    for c in range(4):
        n = np.arange(c, NT, 4, dtype=np.int64)
        cos, sin = trig(n[:, None] * p[None, :], NT)
        sin[:, 0] = np.where(np.arange(NT // 4) % 2 == 0, 1.0, -1.0) * (math.sqrt(0.5) if c % 2 else 1.0)
        both = np.stack([cos.reshape(NT // 4, 4, 128), sin.reshape(NT // 4, 4, 128)], axis=2)
        parts.append(both.transpose(1, 0, 2, 3).reshape(4, NT // 4, 256))
    return np.stack(parts, axis=1).astype(jnp.bfloat16)


@functools.cache
def parting_table():
    lane = np.arange(512)
    return (lane[:, None] == (lane % 128 * 4 + lane // 128)[None, :]).astype(jnp.bfloat16)


@functools.cache
def smooth_tables():
    order = np.concatenate([band_places(), band_mirrors()]).reshape(16, 128)
    tables, use, count = [], [], 0
    for t in range(16):
        near = [np.abs(order[s][:, None] - order[t][None, :]) <= SMOOTH for s in range(16)]
        tiles = [s for s in range(16) if near[s].any()]
        table = np.zeros((6, 128, 128), np.float32)
        for k, s in enumerate(tiles):
            table[k] = near[s]
        count += table.sum()
        tiles += [t] * (len(tiles) % 2)
        same = [k for k, other in enumerate(tables) if (other == table).all()]
        if not same:
            tables.append(table)
        use.append((tiles, same[0] if same else len(tables) - 1))
    f = np.arange(NF)
    assert count == (np.minimum(f + SMOOTH, NF - 1) - np.maximum(f - SMOOTH, 0) + 1).sum()
    return np.stack(tables).reshape(len(tables), 768, 128).astype(jnp.bfloat16), tuple(use)


@functools.cache
def taper_rows():
    f = np.stack([band_places(), band_mirrors()]).astype(np.float64)
    rising = np.minimum(np.minimum(f + 0.5, NF - f - 0.5) / EDGE, 1.0)
    return (np.sin(0.5 * math.pi * rising) ** 2).astype(np.float32)


@functools.cache
def spread_table():
    lane = np.arange(128)
    out = np.zeros((128, 8, 128), np.float32)
    for u in range(8):
        out[:, u] = (lane[:, None] // 16 == u) & (lane[:, None] % 16 == lane[None, :] % 16)
    return out.reshape(128, 1024).astype(jnp.bfloat16)


LAG_ROWS = 272


@functools.cache
def lag_tables():
    p = band_places()
    out = np.zeros((4, LAG_ROWS, HALF), np.float32)
    for odd in range(2):
        m = np.arange(odd, LAGS // 2 + 1, 2, dtype=np.int64)
        cos, sin = trig(m[:, None] * p[None, :], NT)
        out[2 * odd, : len(m)], out[2 * odd + 1, : len(m)] = cos, sin
        if odd:
            out[3, : len(m), 0] = np.rint(trig(m * HALF, NT)[1])
    return out.astype(jnp.bfloat16)


@functools.cache
def turning_tables():
    r = np.arange(256)
    return np.stack([(r[:, None] + r[None, :] == n) for n in (256, 255)]).astype(jnp.bfloat16)


def spectra_kernel(got_ref, part_hbm, smooth_hbm, taper_hbm, spread_hbm, table_hbm, out_ref,
                   part_ref, smooth_ref, taper_ref, spread_ref, table_ref,
                   x_ref, class_ref, re_ref, im_ref, power_ref, sem, more_sem):
    def arrive(k):
        return pltpu.make_async_copy(table_hbm.at[k], table_ref.at[k], sem.at[k])

    whole = [(part_hbm, part_ref), (smooth_hbm, smooth_ref), (taper_hbm, taper_ref), (spread_hbm, spread_ref)]
    whole = [pltpu.make_async_copy(a, b, more_sem.at[n]) for n, (a, b) in enumerate(whole)]
    whole[0].start()
    for k in range(4):
        arrive(k).start()
    for copy in whole[1:]:
        copy.start()
    tags = jnp.transpose(got_ref[:, WIN : WIN + 128].astype(F32))[0:8]
    wanted = lax.broadcasted_iota(jnp.int32, (8, SLOTS), 0) % CH
    pick = (tags == wanted.astype(F32)).astype(F32).astype(BF)
    for s in range(SEGS):
        seg = got_ref[:, s * NT : (s + 1) * NT]
        x_ref[s * 8 : s * 8 + 8, :] = jnp.dot(pick, seg, preferred_element_type=F32)
    whole[0].wait()
    for t in range(NT // 512):
        x = x_ref[:, t * 512 : t * 512 + 512].astype(BF)
        parted = jnp.dot(x, part_ref[...], preferred_element_type=F32).astype(BF)
        for c in range(4):
            class_ref[c, :, t * 128 : t * 128 + 128] = parted[:, c * 128 : c * 128 + 128]

    lane0 = lax.broadcasted_iota(jnp.int32, (64, 128), 1) == 0

    @pl.loop(0, 4)
    def _(k):
        arrive(k).wait()
        sums = [jnp.dot(class_ref[c], table_ref[k, c], preferred_element_type=F32) for c in range(4)]
        c0, c1, c2, c3 = [v[:, :128] for v in sums]
        s0, s1, s2, s3 = [v[:, 128:] for v in sums]
        top = lane0 & (k == 0)
        half, alone = c0 - c2, c3 - c1
        places = [
            (0, k, c0 + c1 + c2 + c3, jnp.where(top, 0.0, s0 + s1 + s2 + s3)),
            (1, k, jnp.where(top, half, c0 + c2 - c1 - c3), jnp.where(top, alone, s1 + s3 - s0 - s2)),
            (0, k + 4, jnp.where(top, s0 + s1 - s3, half - s1 + s3), jnp.where(top, -s2 - s1 - s3, alone - s0 + s2)),
            (1, k + 4, jnp.where(top, s0 - s1 + s3, half + s1 - s3), jnp.where(top, s2 - s1 - s3, alone + s0 - s2)),
        ]
        for h, tile, re, im in places:
            re_ref[h, tile] = re
            im_ref[h, tile] = im
            power = re * re + im * im
            hi = power.astype(BF)
            power_ref[h, tile, 0:64, :] = hi
            power_ref[h, tile, 64:128, :] = (power - hi.astype(F32)).astype(BF)

    for copy in whole[1:]:
        copy.wait()
    use = smooth_tables()[1]
    is_re = (lax.broadcasted_iota(jnp.int32, (64, 128), 0) // CH) % 2 == 0
    lane_seg = lax.broadcasted_iota(jnp.int32, (8, 128), 1) // 16
    for t in range(8):
        halves = []
        for h in range(2):
            tiles, number = use[h * 8 + t]
            near = jnp.concatenate([power_ref[k // 8, k % 8] for k in tiles], axis=1)
            both = jnp.dot(near, smooth_ref[number, : near.shape[1]], preferred_element_type=F32)
            smooth = (both[:64] + both[64:]) * (1.0 / (2 * SMOOTH + 1))
            scale = taper_ref[h : h + 1, t * 128 : t * 128 + 128] * lax.rsqrt(smooth + 1e-06)
            spec = (jnp.where(is_re, re_ref[h, t], im_ref[h, t]) * scale).astype(BF)
            spread = jnp.dot(spec, spread_ref[...], preferred_element_type=F32)
            chunks = []
            for u in range(8):
                chunk = spread[:, u * 128 : u * 128 + 128]
                acc = chunk[0:8]
                for s in range(1, SEGS):
                    acc = jnp.where(lane_seg == s, chunk[s * 8 : s * 8 + 8], acc)
                chunks.append(acc)
            halves.append(chunks)
        for u in range(8):
            rows = jnp.concatenate([halves[0][u], halves[1][u]], axis=0).astype(BF)
            out_ref[(t * 8 + u) * 16 : (t * 8 + u) * 16 + 16, :] = rows


def spectra_of(got):
    vmem = pl.BlockSpec(memory_space=pltpu.VMEM)
    return pl.pallas_call(
        spectra_kernel,
        out_shape=jax.ShapeDtypeStruct((1024, 128), BF),
        in_specs=[vmem] + [pl.BlockSpec(memory_space=pl.ANY)] * 5,
        out_specs=vmem,
        scratch_shapes=[
            pltpu.VMEM((512, 512), BF),
            pltpu.VMEM(smooth_tables()[0].shape, BF),
            pltpu.VMEM((2, HALF), F32),
            pltpu.VMEM((128, 1024), BF),
            pltpu.VMEM((4, 4, NT // 4, 256), BF),
            pltpu.VMEM((64, NT), F32),
            pltpu.VMEM((4, 64, NT // 4), BF),
            pltpu.VMEM((2, 8, 64, 128), F32),
            pltpu.VMEM((2, 8, 64, 128), F32),
            pltpu.VMEM((2, 8, 128, 128), BF),
            pltpu.SemaphoreType.DMA((4,)),
            pltpu.SemaphoreType.DMA((4,)),
        ],
        compiler_params=pltpu.CompilerParams(vmem_limit_bytes=58 * 2**20),
        cost_estimate=pl.CostEstimate(flops=2**30, bytes_accessed=NT * NT // 2, transcendentals=0),
        name="spectra",
    )(got, parting_table(), smooth_tables()[0], taper_rows(), spread_table(), dft_table())


CHUNKS = 4


def pair_kernel(pos_ref, a_hbm, *refs):
    nrow, ncol = 8, 16
    b_hbm, c_hbm, refs = refs[:nrow], refs[nrow : 2 * nrow], refs[nrow:]
    lag_hbm, turn_ref, out_hbm, a_ref, b_ref, lag_ref, x_ref, y_ref, f_ref, o_ref, in_sem, lag_sem, out_sem = refs[nrow:]
    size = 1024 // CHUNKS
    side = pos_ref[1] // 2 % 2

    def arrive(k):
        rows = pl.ds(k * size, size)
        copies = []
        for x in range(4):
            copies.append(
                pltpu.make_async_copy(
                    a_hbm.at[pl.ds(x * 2, 2), rows, :], a_ref.at[pl.ds(x * 4 + side * 2, 2), rows, :],
                    in_sem.at[k, 16 + x]))
        for r in range(8):
            copies.append(
                pltpu.make_async_copy(
                    b_hbm[r].at[rows, :], b_ref.at[pos_ref[2 + r], rows, :], in_sem.at[k, r]))
            copies.append(
                pltpu.make_async_copy(
                    c_hbm[r].at[rows, :], a_ref.at[pos_ref[10 + r], rows, :], in_sem.at[k, 8 + r]))
        return copies

    for k in range(CHUNKS):
        for copy in arrive(k):
            copy.start()
    lag_copy = pltpu.make_async_copy(lag_hbm, lag_ref, lag_sem)
    lag_copy.start()

    sub = lax.broadcasted_iota(jnp.int32, (16, 128), 0)
    lane = lax.broadcasted_iota(jnp.int32, (16, 128), 1)
    diagonal = (lane % GRP == sub).astype(F32).astype(BF)
    first = (lane // CH) % 2 == 0
    swap_sign = jnp.where(sub % 8 < 4, 1.0, -1.0)

    def group(g, special):
        rows = pl.ds(pl.multiple_of(g * 16, 16), 16)
        tiles = [a_ref[d, rows, :] for d in range(ncol)]
        turned = []
        for d in range(ncol):
            v = tiles[d].astype(F32)
            v = jnp.concatenate([pltpu.roll(v[0:8], 4, 0), pltpu.roll(v[8:16], 4, 0)], axis=0)
            turned.append(v * swap_sign)
        own = [b_ref[d, rows, :].astype(F32) for d in range(nrow)]
        prods = []
        for h in range(2):
            left = jnp.concatenate([t.astype(F32)[h * 8 : h * 8 + 8] for t in tiles], axis=0)
            right = jnp.concatenate([t[h * 8 : h * 8 + 8] for t in turned], axis=0)
            w = jnp.concatenate([left, right], axis=1).astype(BF)
            blocks = []
            for d in range(nrow):
                for c in range(CH):
                    r = h * 8 + c
                    re = jnp.broadcast_to(own[d][r : r + 1, :], (16, 128)).astype(BF)
                    im = jnp.broadcast_to(own[d][r + CH : r + CH + 1, :], (16, 128)).astype(BF)
                    blocks.append(jnp.concatenate([re * diagonal, im * diagonal], axis=1))
            lhs = jnp.concatenate(blocks, axis=0)
            prods.append(
                lax.dot_general(lhs, w, (((1,), (1,)), ((), ())), preferred_element_type=F32)
            )
        pairs = nrow * CH // 2
        for jp in range(pairs):
            parts = []
            for h in range(2):
                j = jp // 8 * 16 + jp % 8
                t0 = prods[h][j * 16 : j * 16 + 16]
                t1 = prods[h][(j + 8) * 16 : (j + 8) * 16 + 16]
                re = jnp.where(first, t0, pltpu.roll(t1, 4, 1))
                im = jnp.where(first, pltpu.roll(t0, 124, 1), t1)
                parts += [re, im]
            re0, im0, re1, im1 = parts
            sums = [re0 + re1, im0 - im1, re0 - re1, im0 + im1]
            if special:
                top = sub == 0
                sums = [
                    jnp.where(top, re0, sums[0]),
                    jnp.where(top, re1, sums[1]),
                    jnp.where(top, re0, sums[2]),
                    jnp.where(top, im1, sums[3]),
                ]
            for k in range(4):
                x_ref[k, rows, jp * 128 : jp * 128 + 128] = sums[k].astype(BF)

    @pl.loop(0, CHUNKS)
    def _(k):
        for copy in arrive(k):
            copy.wait()

        for u in range(NGRP // CHUNKS):
            group(k * (NGRP // CHUNKS) + u, False)

    group(0, True)
    lag_copy.wait()

    my_row, my_col = pos_ref[0], pos_ref[1]
    line = lax.broadcasted_iota(jnp.int32, (16, 128), 0)
    place = lax.broadcasted_iota(jnp.int32, (LAG_ROWS, 1), 0)
    alternate = jnp.where(place % 2 == 0, 1.0, -1.0)

    def leave(half, d):
        lines = pl.ds(half * 16, 16)
        return pltpu.make_async_copy(
            o_ref.at[pl.ds(d * CH, CH), lines, :], out_hbm.at[pl.ds(d * CH, CH), lines, :], out_sem.at[half, d])

    for half in range(2):

        @pl.loop(0, 4, unroll=4)
        def _(n):
            cols = pl.ds(pl.multiple_of(half * 1024 + n * 256, 256), 256)
            for odd in range(2):
                size = 256 if odd else LAG_ROWS
                cos = jnp.dot(lag_ref[2 * odd, :size], x_ref[2 * odd, :, cols], preferred_element_type=F32)
                sin = jnp.dot(lag_ref[2 * odd + 1, :size], x_ref[2 * odd + 1, :, cols], preferred_element_type=F32)
                if not odd:
                    cos += alternate * x_ref[1, 0:16, cols].astype(F32)[0:1]
                later = (cos + sin)[:256]
                sooner = cos - sin
                turned = jnp.dot(turn_ref[odd], sooner[:256].astype(BF), preferred_element_type=F32)
                for k in range(2):
                    half_cols = slice(k * 128, k * 128 + 128)
                    y_ref[k, pl.ds(odd, 256, stride=2), :] = turned[:, half_cols]
                    y_ref[k, pl.ds(LAGS // 2 + odd, 256, stride=2), :] = later[:, half_cols]
                    if not odd:
                        y_ref[k, 0:1, :] = sooner[256:257, half_cols]
            for k in range(2):
                at = pl.ds((n * 2 + k) * 129, 128)
                for t in range(LAGS // 128):
                    f_ref[t, at, :] = jnp.transpose(y_ref[k, t * 128 : t * 128 + 128, :])

        @pl.loop(0, ncol)
        def _(d):
            for c in range(CH):
                own = jnp.where(d == my_col, my_row * CH + c, -1)
                drop = line + half * 16 == own
                for t in range(LAGS // 128):
                    v = jnp.concatenate(
                        [f_ref[t, pl.ds(d * 8 + e * 4 + c, 8, stride=129), :] for e in range(2)], axis=0)
                    v = jnp.where(drop, 0.0, v * (1.0 / math.sqrt(SEGS * NF)))
                    o_ref[d * CH + c, half * 16 : half * 16 + 16, t * 128 : t * 128 + 128] = v.astype(BF)
            leave(half, d).start()

    for half in range(2):
        for d in range(ncol):
            leave(half, d).wait()


def pairs_of(pos, a, b, c):
    nrow, ncol = len(b), a.shape[0] + len(c)
    assert nrow == 8 and ncol == 16
    anywhere = pl.BlockSpec(memory_space=pl.ANY)
    return pl.pallas_call(
        pair_kernel,
        out_shape=jax.ShapeDtypeStruct((ncol * CH, nrow * CH, LAGS), BF),
        in_specs=[pl.BlockSpec(memory_space=pltpu.SMEM)] + [anywhere] * (2 * nrow + 2)
        + [pl.BlockSpec(memory_space=pltpu.VMEM)],
        out_specs=anywhere,
        scratch_shapes=[
            pltpu.VMEM((ncol, 1024, 128), BF),
            pltpu.VMEM((nrow, 1024, 128), BF),
            pltpu.VMEM((4, LAG_ROWS, HALF), BF),
            pltpu.VMEM((4, HALF, 2048), BF),
            pltpu.VMEM((2, LAGS, 128), F32),
            pltpu.VMEM((LAGS // 128, 8 * 129 + 8, 128), F32),
            pltpu.VMEM((ncol * CH, nrow * CH, LAGS), BF),
            pltpu.SemaphoreType.DMA((CHUNKS, 20)),
            pltpu.SemaphoreType.DMA,
            pltpu.SemaphoreType.DMA((2, ncol)),
        ],
        compiler_params=pltpu.CompilerParams(vmem_limit_bytes=52 * 2**20),
        cost_estimate=pl.CostEstimate(flops=2**34, bytes_accessed=16 * 2**20, transcendentals=0),
        name="pairs",
    )(pos, a, *b, *c, lag_tables(), turning_tables())


def over_row(own, my_row):
    def move(block, step, across=0):
        pairs = [(y * 4 + z, (y ^ across) * 4 + (z + step) % 4) for y in range(2) for z in range(4)]
        return lax.ppermute(block, "row", pairs)

    y, z = my_row // 4, my_row % 4
    index = lambda step, across: (y ^ across) * 4 + (z + step) % 4
    other = move(own, 0, 1)
    left, right = move(own, 1), move(own, -1)
    other_left, other_right = move(other, 1), move(other, -1)
    far, other_far = move(left, 1), move(other_right, -1)
    blocks = [own, other, left, right, other_left, other_right, far, other_far]
    rows = [
        index(0, 0), index(0, 1), index(-1, 0), index(1, 0),
        index(-1, 1), index(1, 1), index(2, 0), index(2, 1),
    ]
    return blocks, rows


def over_col(own, my_col):
    def move(block, step=0, across=0, core=0):
        pairs = [
            (x * 4 + y * 2 + c, (x + step) % 4 * 4 + (y ^ across) * 2 + (c ^ core))
            for x in range(4) for y in range(2) for c in range(2)]
        return lax.ppermute(block, "col", pairs)

    x, y, core = my_col // 4, my_col // 2 % 2, my_col % 2
    near = move(own, across=1)
    left, right = move(near, 1), move(near, -1)
    blocks = [near, left, right, move(left, 1)]
    cols = [(x + step) % 4 * 4 + (y ^ 1) * 2 for step in (0, -1, 1, 2)]
    blocks += [move(v, core=1) for v in blocks]
    return blocks, [c + core for c in cols] + [c + (core ^ 1) for c in cols]


def local(strain, file_channels, file_counts, window_start):
    nrow, ncol = lax.axis_size("row"), lax.axis_size("col")
    my_row, my_col = lax.axis_index("row"), lax.axis_index("col")
    window = lax.dynamic_slice_in_dim(strain, window_start[0], WIN, 1)
    slot = jnp.arange(SLOTS, dtype=jnp.int32)
    live = slot < file_counts[0]
    owner = jnp.where(live, file_channels // CH // ncol, -1)
    place = file_channels % CH
    before = (owner[None, :] == owner[:, None]) & (slot[None, :] < slot[:, None])
    rank = jnp.sum(before.astype(jnp.int32), axis=1)
    lines = jnp.arange(2 * nrow, dtype=jnp.int32)
    choose = (owner[None, :] == lines[:, None] // 2) & (rank[None, :] == lines[:, None] % 2)
    labels = jnp.sum(jnp.where(choose, place[None, :] + 1, 0), axis=1) - 1
    bundle = jnp.dot(choose.astype(BF), window, preferred_element_type=F32).astype(BF)
    tags = jnp.broadcast_to(labels.astype(BF)[:, None], (2 * nrow, 128))
    sent = jnp.concatenate([bundle, tags], axis=1).reshape(nrow, 2, WIN + 128)
    got = lax.all_to_all(sent, "row", 0, 0).reshape(2 * nrow, WIN + 128)
    own = spectra_of(got)
    rings = [[x * 4 + y * 2 + core for x in range(4) for core in range(2)] for y in range(2)]
    a = lax.all_gather(own, "col", axis=0, axis_index_groups=rings)
    c, cols = over_col(own, my_col)
    b, rows = over_row(own, my_row)
    pos = jnp.stack([my_row, my_col, *rows, *cols]).astype(jnp.int32)
    return pairs_of(pos, a, b, c)


def solution(mesh):
    placed = (P(("row", "col"), None), P(("row", "col")), P(("row", "col")), P(("row", "col")))
    return jax.shard_map(
        local, mesh=mesh, in_specs=placed, out_specs=P("row", "col", None), check_vma=False
    )
```

```python
import functools
import math

import jax
import jax.numpy as jnp
import numpy as np
from jax import lax
from jax.experimental import pallas as pl
from jax.experimental.pallas import tpu as pltpu
from jax.sharding import PartitionSpec as P

NF = 2048
NT = 4096
LAGS = 1024
SEGS = 8
CH = 4
SLOTS = 16
SMOOTH = 32
EDGE = 128
WIN = SEGS * NT
HALF = NF // 2
QUARTER = NF // 4
GRP = 16
NGRP = HALF // GRP
BF = jnp.bfloat16
F32 = jnp.float32


def band_places():
    p = np.arange(QUARTER, dtype=np.int64)
    return np.concatenate([p, np.where(p == 0, QUARTER, HALF - p)])


def band_mirrors():
    f = band_places()
    return np.where(f == 0, HALF, NF - f)


def trig(product, size):
    angle = (product % size).astype(np.float32) * np.float32(2.0 * math.pi / size)
    return np.cos(angle.astype(np.float64)), -np.sin(angle.astype(np.float64))


@functools.cache
def dft_table():
    p = np.arange(QUARTER, dtype=np.int64)
    parts = []
    for c in range(4):
        n = np.arange(c, NT, 4, dtype=np.int64)
        cos, sin = trig(n[:, None] * p[None, :], NT)
        sin[:, 0] = np.where(np.arange(NT // 4) % 2 == 0, 1.0, -1.0) * (math.sqrt(0.5) if c % 2 else 1.0)
        both = np.stack([cos.reshape(NT // 4, 4, 128), sin.reshape(NT // 4, 4, 128)], axis=2)
        parts.append(both.transpose(1, 0, 2, 3).reshape(4, NT // 4, 256))
    return np.stack(parts, axis=1).astype(jnp.bfloat16)


@functools.cache
def parting_table():
    lane = np.arange(512)
    return (lane[:, None] == (lane % 128 * 4 + lane // 128)[None, :]).astype(jnp.bfloat16)


@functools.cache
def smooth_tables():
    order = np.concatenate([band_places(), band_mirrors()]).reshape(16, 128)
    tables, use, count = [], [], 0
    for t in range(16):
        near = [np.abs(order[s][:, None] - order[t][None, :]) <= SMOOTH for s in range(16)]
        tiles = [s for s in range(16) if near[s].any()]
        table = np.zeros((6, 128, 128), np.float32)
        for k, s in enumerate(tiles):
            table[k] = near[s]
        count += table.sum()
        tiles += [t] * (len(tiles) % 2)
        same = [k for k, other in enumerate(tables) if (other == table).all()]
        if not same:
            tables.append(table)
        use.append((tiles, same[0] if same else len(tables) - 1))
    f = np.arange(NF)
    assert count == (np.minimum(f + SMOOTH, NF - 1) - np.maximum(f - SMOOTH, 0) + 1).sum()
    return np.stack(tables).reshape(len(tables), 768, 128).astype(jnp.bfloat16), tuple(use)


@functools.cache
def taper_rows():
    f = np.stack([band_places(), band_mirrors()]).astype(np.float64)
    rising = np.minimum(np.minimum(f + 0.5, NF - f - 0.5) / EDGE, 1.0)
    return (np.sin(0.5 * math.pi * rising) ** 2).astype(np.float32)


@functools.cache
def spread_table():
    lane = np.arange(128)
    out = np.zeros((128, 8, 128), np.float32)
    for u in range(8):
        out[:, u] = (lane[:, None] // 16 == u) & (lane[:, None] % 16 == lane[None, :] % 16)
    return out.reshape(128, 1024).astype(jnp.bfloat16)


LAG_ROWS = 272


@functools.cache
def lag_tables():
    p = band_places()
    out = np.zeros((4, LAG_ROWS, HALF), np.float32)
    for odd in range(2):
        m = np.arange(odd, LAGS // 2 + 1, 2, dtype=np.int64)
        cos, sin = trig(m[:, None] * p[None, :], NT)
        out[2 * odd, : len(m)], out[2 * odd + 1, : len(m)] = cos, sin
        if odd:
            out[3, : len(m), 0] = np.rint(trig(m * HALF, NT)[1])
    return out.astype(jnp.bfloat16)


@functools.cache
def turning_tables():
    r = np.arange(256)
    return np.stack([(r[:, None] + r[None, :] == n) for n in (256, 255)]).astype(jnp.bfloat16)


def spectra_kernel(got_ref, part_hbm, smooth_hbm, taper_hbm, spread_hbm, table_hbm, out_ref,
                   part_ref, smooth_ref, taper_ref, spread_ref, table_ref,
                   x_ref, class_ref, re_ref, im_ref, power_ref, sem, more_sem):
    def arrive(k):
        return pltpu.make_async_copy(table_hbm.at[k], table_ref.at[k], sem.at[k])

    whole = [(part_hbm, part_ref), (smooth_hbm, smooth_ref), (taper_hbm, taper_ref), (spread_hbm, spread_ref)]
    whole = [pltpu.make_async_copy(a, b, more_sem.at[n]) for n, (a, b) in enumerate(whole)]
    whole[0].start()
    for k in range(4):
        arrive(k).start()
    for copy in whole[1:]:
        copy.start()
    tags = jnp.transpose(got_ref[:, WIN : WIN + 128].astype(F32))[0:8]
    wanted = lax.broadcasted_iota(jnp.int32, (8, SLOTS), 0) % CH
    pick = (tags == wanted.astype(F32)).astype(F32).astype(BF)
    for s in range(SEGS):
        seg = got_ref[:, s * NT : (s + 1) * NT]
        x_ref[s * 8 : s * 8 + 8, :] = jnp.dot(pick, seg, preferred_element_type=F32)
    whole[0].wait()
    for t in range(NT // 512):
        x = x_ref[:, t * 512 : t * 512 + 512].astype(BF)
        parted = jnp.dot(x, part_ref[...], preferred_element_type=F32).astype(BF)
        for c in range(4):
            class_ref[c, :, t * 128 : t * 128 + 128] = parted[:, c * 128 : c * 128 + 128]

    lane0 = lax.broadcasted_iota(jnp.int32, (64, 128), 1) == 0

    @pl.loop(0, 4)
    def _(k):
        arrive(k).wait()
        sums = [jnp.dot(class_ref[c], table_ref[k, c], preferred_element_type=F32) for c in range(4)]
        c0, c1, c2, c3 = [v[:, :128] for v in sums]
        s0, s1, s2, s3 = [v[:, 128:] for v in sums]
        top = lane0 & (k == 0)
        half, alone = c0 - c2, c3 - c1
        places = [
            (0, k, c0 + c1 + c2 + c3, jnp.where(top, 0.0, s0 + s1 + s2 + s3)),
            (1, k, jnp.where(top, half, c0 + c2 - c1 - c3), jnp.where(top, alone, s1 + s3 - s0 - s2)),
            (0, k + 4, jnp.where(top, s0 + s1 - s3, half - s1 + s3), jnp.where(top, -s2 - s1 - s3, alone - s0 + s2)),
            (1, k + 4, jnp.where(top, s0 - s1 + s3, half + s1 - s3), jnp.where(top, s2 - s1 - s3, alone + s0 - s2)),
        ]
        for h, tile, re, im in places:
            re_ref[h, tile] = re
            im_ref[h, tile] = im
            power = re * re + im * im
            hi = power.astype(BF)
            power_ref[h, tile, 0:64, :] = hi
            power_ref[h, tile, 64:128, :] = (power - hi.astype(F32)).astype(BF)

    for copy in whole[1:]:
        copy.wait()
    use = smooth_tables()[1]
    is_re = (lax.broadcasted_iota(jnp.int32, (64, 128), 0) // CH) % 2 == 0
    lane_seg = lax.broadcasted_iota(jnp.int32, (8, 128), 1) // 16
    for t in range(8):
        halves = []
        for h in range(2):
            tiles, number = use[h * 8 + t]
            near = jnp.concatenate([power_ref[k // 8, k % 8] for k in tiles], axis=1)
            both = jnp.dot(near, smooth_ref[number, : near.shape[1]], preferred_element_type=F32)
            smooth = (both[:64] + both[64:]) * (1.0 / (2 * SMOOTH + 1))
            scale = taper_ref[h : h + 1, t * 128 : t * 128 + 128] * lax.rsqrt(smooth + 1e-06)
            spec = (jnp.where(is_re, re_ref[h, t], im_ref[h, t]) * scale).astype(BF)
            spread = jnp.dot(spec, spread_ref[...], preferred_element_type=F32)
            chunks = []
            for u in range(8):
                chunk = spread[:, u * 128 : u * 128 + 128]
                acc = chunk[0:8]
                for s in range(1, SEGS):
                    acc = jnp.where(lane_seg == s, chunk[s * 8 : s * 8 + 8], acc)
                chunks.append(acc)
            halves.append(chunks)
        for u in range(8):
            rows = jnp.concatenate([halves[0][u], halves[1][u]], axis=0).astype(BF)
            out_ref[(t * 8 + u) * 16 : (t * 8 + u) * 16 + 16, :] = rows


def spectra_of(got):
    vmem = pl.BlockSpec(memory_space=pltpu.VMEM)
    return pl.pallas_call(
        spectra_kernel,
        out_shape=jax.ShapeDtypeStruct((1024, 128), BF),
        in_specs=[vmem] + [pl.BlockSpec(memory_space=pl.ANY)] * 5,
        out_specs=vmem,
        scratch_shapes=[
            pltpu.VMEM((512, 512), BF),
            pltpu.VMEM(smooth_tables()[0].shape, BF),
            pltpu.VMEM((2, HALF), F32),
            pltpu.VMEM((128, 1024), BF),
            pltpu.VMEM((4, 4, NT // 4, 256), BF),
            pltpu.VMEM((64, NT), F32),
            pltpu.VMEM((4, 64, NT // 4), BF),
            pltpu.VMEM((2, 8, 64, 128), F32),
            pltpu.VMEM((2, 8, 64, 128), F32),
            pltpu.VMEM((2, 8, 128, 128), BF),
            pltpu.SemaphoreType.DMA((4,)),
            pltpu.SemaphoreType.DMA((4,)),
        ],
        compiler_params=pltpu.CompilerParams(vmem_limit_bytes=58 * 2**20),
        cost_estimate=pl.CostEstimate(flops=2**30, bytes_accessed=NT * NT // 2, transcendentals=0),
        name="spectra",
    )(got, parting_table(), smooth_tables()[0], taper_rows(), spread_table(), dft_table())


CHUNKS = 4


def pair_kernel(pos_ref, a_hbm, *refs):
    nrow, ncol = 8, 16
    b_hbm, c_hbm, refs = refs[:nrow], refs[nrow : 2 * nrow], refs[nrow:]
    lag_hbm, turn_ref, out_hbm, a_ref, b_ref, lag_ref, x_ref, y_ref, f_ref, o_ref, in_sem, lag_sem, out_sem = refs[nrow:]
    size = 1024 // CHUNKS
    side = pos_ref[1] // 2 % 2

    def arrive(k):
        rows = pl.ds(k * size, size)
        copies = []
        for x in range(4):
            copies.append(
                pltpu.make_async_copy(
                    a_hbm.at[pl.ds(x * 2, 2), rows, :], a_ref.at[pl.ds(x * 4 + side * 2, 2), rows, :],
                    in_sem.at[k, 16 + x]))
        for r in range(8):
            copies.append(
                pltpu.make_async_copy(
                    b_hbm[r].at[rows, :], b_ref.at[pos_ref[2 + r], rows, :], in_sem.at[k, r]))
            copies.append(
                pltpu.make_async_copy(
                    c_hbm[r].at[rows, :], a_ref.at[pos_ref[10 + r], rows, :], in_sem.at[k, 8 + r]))
        return copies

    for k in range(CHUNKS):
        for copy in arrive(k):
            copy.start()
    lag_copy = pltpu.make_async_copy(lag_hbm, lag_ref, lag_sem)
    lag_copy.start()

    sub = lax.broadcasted_iota(jnp.int32, (16, 128), 0)
    lane = lax.broadcasted_iota(jnp.int32, (16, 128), 1)
    diagonal = (lane % GRP == sub).astype(F32).astype(BF)
    first = (lane // CH) % 2 == 0
    swap_sign = jnp.where(sub % 8 < 4, 1.0, -1.0)

    def group(g, special):
        rows = pl.ds(pl.multiple_of(g * 16, 16), 16)
        tiles = [a_ref[d, rows, :] for d in range(ncol)]
        turned = []
        for d in range(ncol):
            v = tiles[d].astype(F32)
            v = jnp.concatenate([pltpu.roll(v[0:8], 4, 0), pltpu.roll(v[8:16], 4, 0)], axis=0)
            turned.append(v * swap_sign)
        own = [b_ref[d, rows, :].astype(F32) for d in range(nrow)]
        prods = []
        for h in range(2):
            left = jnp.concatenate([t.astype(F32)[h * 8 : h * 8 + 8] for t in tiles], axis=0)
            right = jnp.concatenate([t[h * 8 : h * 8 + 8] for t in turned], axis=0)
            w = jnp.concatenate([left, right], axis=1).astype(BF)
            blocks = []
            for d in range(nrow):
                for c in range(CH):
                    r = h * 8 + c
                    re = jnp.broadcast_to(own[d][r : r + 1, :], (16, 128)).astype(BF)
                    im = jnp.broadcast_to(own[d][r + CH : r + CH + 1, :], (16, 128)).astype(BF)
                    blocks.append(jnp.concatenate([re * diagonal, im * diagonal], axis=1))
            lhs = jnp.concatenate(blocks, axis=0)
            prods.append(
                lax.dot_general(lhs, w, (((1,), (1,)), ((), ())), preferred_element_type=F32)
            )
        pairs = nrow * CH // 2
        for jp in range(pairs):
            parts = []
            for h in range(2):
                j = jp // 8 * 16 + jp % 8
                t0 = prods[h][j * 16 : j * 16 + 16]
                t1 = prods[h][(j + 8) * 16 : (j + 8) * 16 + 16]
                re = jnp.where(first, t0, pltpu.roll(t1, 4, 1))
                im = jnp.where(first, pltpu.roll(t0, 124, 1), t1)
                parts += [re, im]
            re0, im0, re1, im1 = parts
            sums = [re0 + re1, im0 - im1, re0 - re1, im0 + im1]
            if special:
                top = sub == 0
                sums = [
                    jnp.where(top, re0, sums[0]),
                    jnp.where(top, re1, sums[1]),
                    jnp.where(top, re0, sums[2]),
                    jnp.where(top, im1, sums[3]),
                ]
            for k in range(4):
                x_ref[k, rows, jp * 128 : jp * 128 + 128] = sums[k].astype(BF)

    @pl.loop(0, CHUNKS)
    def _(k):
        for copy in arrive(k):
            copy.wait()

        for u in range(NGRP // CHUNKS):
            group(k * (NGRP // CHUNKS) + u, False)

    group(0, True)
    lag_copy.wait()

    my_row, my_col = pos_ref[0], pos_ref[1]
    line = lax.broadcasted_iota(jnp.int32, (16, 128), 0)
    place = lax.broadcasted_iota(jnp.int32, (LAG_ROWS, 1), 0)
    alternate = jnp.where(place % 2 == 0, 1.0, -1.0)

    def leave(half, d):
        lines = pl.ds(half * 16, 16)
        return pltpu.make_async_copy(
            o_ref.at[pl.ds(d * CH, CH), lines, :], out_hbm.at[pl.ds(d * CH, CH), lines, :], out_sem.at[half, d])

    for half in range(2):

        @pl.loop(0, 4, unroll=4)
        def _(n):
            cols = pl.ds(pl.multiple_of(half * 1024 + n * 256, 256), 256)
            for odd in range(2):
                size = 256 if odd else LAG_ROWS
                cos = jnp.dot(lag_ref[2 * odd, :size], x_ref[2 * odd, :, cols], preferred_element_type=F32)
                sin = jnp.dot(lag_ref[2 * odd + 1, :size], x_ref[2 * odd + 1, :, cols], preferred_element_type=F32)
                if not odd:
                    cos += alternate * x_ref[1, 0:16, cols].astype(F32)[0:1]
                later = (cos + sin)[:256]
                sooner = cos - sin
                turned = jnp.dot(turn_ref[odd], sooner[:256].astype(BF), preferred_element_type=F32)
                for k in range(2):
                    half_cols = slice(k * 128, k * 128 + 128)
                    y_ref[k, pl.ds(odd, 256, stride=2), :] = turned[:, half_cols]
                    y_ref[k, pl.ds(LAGS // 2 + odd, 256, stride=2), :] = later[:, half_cols]
                    if not odd:
                        y_ref[k, 0:1, :] = sooner[256:257, half_cols]
            for k in range(2):
                at = pl.ds((n * 2 + k) * 129, 128)
                for t in range(LAGS // 128):
                    f_ref[t, at, :] = jnp.transpose(y_ref[k, t * 128 : t * 128 + 128, :])

        @pl.loop(0, ncol)
        def _(d):
            for c in range(CH):
                own = jnp.where(d == my_col, my_row * CH + c, -1)
                drop = line + half * 16 == own
                for t in range(LAGS // 128):
                    v = jnp.concatenate(
                        [f_ref[t, pl.ds(d * 8 + e * 4 + c, 8, stride=129), :] for e in range(2)], axis=0)
                    v = jnp.where(drop, 0.0, v * (1.0 / math.sqrt(SEGS * NF)))
                    o_ref[d * CH + c, half * 16 : half * 16 + 16, t * 128 : t * 128 + 128] = v.astype(BF)
            leave(half, d).start()

    for half in range(2):
        for d in range(ncol):
            leave(half, d).wait()


def pairs_of(pos, a, b, c):
    nrow, ncol = len(b), a.shape[0] + len(c)
    assert nrow == 8 and ncol == 16
    anywhere = pl.BlockSpec(memory_space=pl.ANY)
    return pl.pallas_call(
        pair_kernel,
        out_shape=jax.ShapeDtypeStruct((ncol * CH, nrow * CH, LAGS), BF),
        in_specs=[pl.BlockSpec(memory_space=pltpu.SMEM)] + [anywhere] * (2 * nrow + 2)
        + [pl.BlockSpec(memory_space=pltpu.VMEM)],
        out_specs=anywhere,
        scratch_shapes=[
            pltpu.VMEM((ncol, 1024, 128), BF),
            pltpu.VMEM((nrow, 1024, 128), BF),
            pltpu.VMEM((4, LAG_ROWS, HALF), BF),
            pltpu.VMEM((4, HALF, 2048), BF),
            pltpu.VMEM((2, LAGS, 128), F32),
            pltpu.VMEM((LAGS // 128, 8 * 129 + 8, 128), F32),
            pltpu.VMEM((ncol * CH, nrow * CH, LAGS), BF),
            pltpu.SemaphoreType.DMA((CHUNKS, 20)),
            pltpu.SemaphoreType.DMA,
            pltpu.SemaphoreType.DMA((2, ncol)),
        ],
        compiler_params=pltpu.CompilerParams(vmem_limit_bytes=60 * 2**20),
        cost_estimate=pl.CostEstimate(flops=2**34, bytes_accessed=16 * 2**20, transcendentals=0),
        name="pairs",
    )(pos, a, *b, *c, lag_tables(), turning_tables())


def over_row(own, my_row):
    def move(block, step, across=0):
        pairs = [(y * 4 + z, (y ^ across) * 4 + (z + step) % 4) for y in range(2) for z in range(4)]
        return lax.ppermute(block, "row", pairs)

    y, z = my_row // 4, my_row % 4
    index = lambda step, across: (y ^ across) * 4 + (z + step) % 4
    other = move(own, 0, 1)
    left, right = move(own, 1), move(own, -1)
    other_left, other_right = move(other, 1), move(other, -1)
    far, other_far = move(left, 1), move(other_right, -1)
    blocks = [own, other, left, right, other_left, other_right, far, other_far]
    rows = [
        index(0, 0), index(0, 1), index(-1, 0), index(1, 0),
        index(-1, 1), index(1, 1), index(2, 0), index(2, 1),
    ]
    return blocks, rows


def over_col(own, my_col):
    def move(block, step=0, across=0, core=0):
        pairs = [
            (x * 4 + y * 2 + c, (x + step) % 4 * 4 + (y ^ across) * 2 + (c ^ core))
            for x in range(4) for y in range(2) for c in range(2)]
        return lax.ppermute(block, "col", pairs)

    x, y, core = my_col // 4, my_col // 2 % 2, my_col % 2
    near = move(own, across=1)
    left, right = move(near, 1), move(near, -1)
    blocks = [near, left, right, move(left, 1)]
    cols = [(x + step) % 4 * 4 + (y ^ 1) * 2 for step in (0, -1, 1, 2)]
    blocks += [move(v, core=1) for v in blocks]
    return blocks, [c + core for c in cols] + [c + (core ^ 1) for c in cols]


def local(strain, file_channels, file_counts, window_start):
    nrow, ncol = lax.axis_size("row"), lax.axis_size("col")
    my_row, my_col = lax.axis_index("row"), lax.axis_index("col")
    window = lax.dynamic_slice_in_dim(strain, window_start[0], WIN, 1)
    slot = jnp.arange(SLOTS, dtype=jnp.int32)
    live = slot < file_counts[0]
    owner = jnp.where(live, file_channels // CH // ncol, -1)
    place = file_channels % CH
    before = (owner[None, :] == owner[:, None]) & (slot[None, :] < slot[:, None])
    rank = jnp.sum(before.astype(jnp.int32), axis=1)
    lines = jnp.arange(2 * nrow, dtype=jnp.int32)
    choose = (owner[None, :] == lines[:, None] // 2) & (rank[None, :] == lines[:, None] % 2)
    labels = jnp.sum(jnp.where(choose, place[None, :] + 1, 0), axis=1) - 1
    bundle = jnp.dot(choose.astype(BF), window, preferred_element_type=F32).astype(BF)
    tags = jnp.broadcast_to(labels.astype(BF)[:, None], (2 * nrow, 128))
    sent = jnp.concatenate([bundle, tags], axis=1).reshape(nrow, 2, WIN + 128)
    got = lax.all_to_all(sent, "row", 0, 0).reshape(2 * nrow, WIN + 128)
    own = spectra_of(got)
    rings = [[x * 4 + y * 2 + core for x in range(4) for core in range(2)] for y in range(2)]
    a = lax.all_gather(own, "col", axis=0, axis_index_groups=rings)
    c, cols = over_col(own, my_col)
    b, rows = over_row(own, my_row)
    pos = jnp.stack([my_row, my_col, *rows, *cols]).astype(jnp.int32)
    return pairs_of(pos, a, b, c)


def solution(mesh):
    placed = (P(("row", "col"), None), P(("row", "col")), P(("row", "col")), P(("row", "col")))
    return jax.shard_map(
        local, mesh=mesh, in_specs=placed, out_specs=P("row", "col", None), check_vma=False
    )
```

```python
import functools
import math

import jax
import jax.numpy as jnp
import numpy as np
from jax import lax
from jax.experimental import pallas as pl
from jax.experimental.pallas import tpu as pltpu
from jax.sharding import PartitionSpec as P

NF = 2048
NT = 4096
LAGS = 1024
SEGS = 8
CH = 4
SLOTS = 16
SMOOTH = 32
EDGE = 128
WIN = SEGS * NT
HALF = NF // 2
QUARTER = NF // 4
GRP = 16
NGRP = HALF // GRP
BF = jnp.bfloat16
F32 = jnp.float32


def band_places():
    p = np.arange(QUARTER, dtype=np.int64)
    return np.concatenate([p, np.where(p == 0, QUARTER, HALF - p)])


def band_mirrors():
    f = band_places()
    return np.where(f == 0, HALF, NF - f)


def trig(product, size):
    angle = (product % size).astype(np.float32) * np.float32(2.0 * math.pi / size)
    return np.cos(angle.astype(np.float64)), -np.sin(angle.astype(np.float64))


@functools.cache
def dft_table():
    p = np.arange(QUARTER, dtype=np.int64)
    parts = []
    for c in range(4):
        n = np.arange(c, NT, 4, dtype=np.int64)
        cos, sin = trig(n[:, None] * p[None, :], NT)
        sin[:, 0] = np.where(np.arange(NT // 4) % 2 == 0, 1.0, -1.0) * (math.sqrt(0.5) if c % 2 else 1.0)
        both = np.stack([cos.reshape(NT // 4, 4, 128), sin.reshape(NT // 4, 4, 128)], axis=2)
        parts.append(both.transpose(1, 0, 2, 3).reshape(4, NT // 4, 256))
    return np.stack(parts, axis=1).astype(jnp.bfloat16)


@functools.cache
def parting_table():
    lane = np.arange(512)
    return (lane[:, None] == (lane % 128 * 4 + lane // 128)[None, :]).astype(jnp.bfloat16)


@functools.cache
def smooth_tables():
    order = np.concatenate([band_places(), band_mirrors()]).reshape(16, 128)
    tables, use, count = [], [], 0
    for t in range(16):
        near = [np.abs(order[s][:, None] - order[t][None, :]) <= SMOOTH for s in range(16)]
        tiles = [s for s in range(16) if near[s].any()]
        table = np.zeros((6, 128, 128), np.float32)
        for k, s in enumerate(tiles):
            table[k] = near[s]
        count += table.sum()
        tiles += [t] * (len(tiles) % 2)
        same = [k for k, other in enumerate(tables) if (other == table).all()]
        if not same:
            tables.append(table)
        use.append((tiles, same[0] if same else len(tables) - 1))
    f = np.arange(NF)
    assert count == (np.minimum(f + SMOOTH, NF - 1) - np.maximum(f - SMOOTH, 0) + 1).sum()
    return np.stack(tables).reshape(len(tables), 768, 128).astype(jnp.bfloat16), tuple(use)


@functools.cache
def taper_rows():
    f = np.stack([band_places(), band_mirrors()]).astype(np.float64)
    rising = np.minimum(np.minimum(f + 0.5, NF - f - 0.5) / EDGE, 1.0)
    return (np.sin(0.5 * math.pi * rising) ** 2).astype(np.float32)


@functools.cache
def spread_table():
    lane = np.arange(128)
    out = np.zeros((128, 8, 128), np.float32)
    for u in range(8):
        out[:, u] = (lane[:, None] // 16 == u) & (lane[:, None] % 16 == lane[None, :] % 16)
    return out.reshape(128, 1024).astype(jnp.bfloat16)


LAG_ROWS = 272


@functools.cache
def lag_tables():
    p = band_places()
    out = np.zeros((4, LAG_ROWS, HALF), np.float32)
    for odd in range(2):
        m = np.arange(odd, LAGS // 2 + 1, 2, dtype=np.int64)
        cos, sin = trig(m[:, None] * p[None, :], NT)
        out[2 * odd, : len(m)], out[2 * odd + 1, : len(m)] = cos, sin
        if odd:
            out[3, : len(m), 0] = np.rint(trig(m * HALF, NT)[1])
    return out.astype(jnp.bfloat16)


@functools.cache
def turning_tables():
    r = np.arange(256)
    return np.stack([(r[:, None] + r[None, :] == n) for n in (256, 255)]).astype(jnp.bfloat16)


def spectra_kernel(got_ref, part_hbm, smooth_hbm, taper_hbm, spread_hbm, table_hbm, out_ref,
                   part_ref, smooth_ref, taper_ref, spread_ref, table_ref,
                   x_ref, class_ref, re_ref, im_ref, power_ref, sem, more_sem):
    def arrive(k):
        return pltpu.make_async_copy(table_hbm.at[k], table_ref.at[k], sem.at[k])

    whole = [(part_hbm, part_ref), (smooth_hbm, smooth_ref), (taper_hbm, taper_ref), (spread_hbm, spread_ref)]
    whole = [pltpu.make_async_copy(a, b, more_sem.at[n]) for n, (a, b) in enumerate(whole)]
    whole[0].start()
    for k in range(4):
        arrive(k).start()
    for copy in whole[1:]:
        copy.start()
    tags = jnp.transpose(got_ref[:, WIN : WIN + 128].astype(F32))[0:8]
    wanted = lax.broadcasted_iota(jnp.int32, (8, SLOTS), 0) % CH
    pick = (tags == wanted.astype(F32)).astype(F32).astype(BF)
    for s in range(SEGS):
        seg = got_ref[:, s * NT : (s + 1) * NT]
        x_ref[s * 8 : s * 8 + 8, :] = jnp.dot(pick, seg, preferred_element_type=F32)
    whole[0].wait()
    for t in range(NT // 512):
        x = x_ref[:, t * 512 : t * 512 + 512].astype(BF)
        parted = jnp.dot(x, part_ref[...], preferred_element_type=F32).astype(BF)
        for c in range(4):
            class_ref[c, :, t * 128 : t * 128 + 128] = parted[:, c * 128 : c * 128 + 128]

    lane0 = lax.broadcasted_iota(jnp.int32, (64, 128), 1) == 0

    @pl.loop(0, 4)
    def _(k):
        arrive(k).wait()
        sums = [jnp.dot(class_ref[c], table_ref[k, c], preferred_element_type=F32) for c in range(4)]
        c0, c1, c2, c3 = [v[:, :128] for v in sums]
        s0, s1, s2, s3 = [v[:, 128:] for v in sums]
        top = lane0 & (k == 0)
        half, alone = c0 - c2, c3 - c1
        places = [
            (0, k, c0 + c1 + c2 + c3, jnp.where(top, 0.0, s0 + s1 + s2 + s3)),
            (1, k, jnp.where(top, half, c0 + c2 - c1 - c3), jnp.where(top, alone, s1 + s3 - s0 - s2)),
            (0, k + 4, jnp.where(top, s0 + s1 - s3, half - s1 + s3), jnp.where(top, -s2 - s1 - s3, alone - s0 + s2)),
            (1, k + 4, jnp.where(top, s0 - s1 + s3, half + s1 - s3), jnp.where(top, s2 - s1 - s3, alone + s0 - s2)),
        ]
        for h, tile, re, im in places:
            re_ref[h, tile] = re
            im_ref[h, tile] = im
            power = re * re + im * im
            hi = power.astype(BF)
            power_ref[h, tile, 0:64, :] = hi
            power_ref[h, tile, 64:128, :] = (power - hi.astype(F32)).astype(BF)

    for copy in whole[1:]:
        copy.wait()
    use = smooth_tables()[1]
    is_re = (lax.broadcasted_iota(jnp.int32, (64, 128), 0) // CH) % 2 == 0
    lane_seg = lax.broadcasted_iota(jnp.int32, (8, 128), 1) // 16
    for t in range(8):
        halves = []
        for h in range(2):
            tiles, number = use[h * 8 + t]
            near = jnp.concatenate([power_ref[k // 8, k % 8] for k in tiles], axis=1)
            both = jnp.dot(near, smooth_ref[number, : near.shape[1]], preferred_element_type=F32)
            smooth = (both[:64] + both[64:]) * (1.0 / (2 * SMOOTH + 1))
            scale = taper_ref[h : h + 1, t * 128 : t * 128 + 128] * lax.rsqrt(smooth + 1e-06)
            spec = (jnp.where(is_re, re_ref[h, t], im_ref[h, t]) * scale).astype(BF)
            spread = jnp.dot(spec, spread_ref[...], preferred_element_type=F32)
            chunks = []
            for u in range(8):
                chunk = spread[:, u * 128 : u * 128 + 128]
                acc = chunk[0:8]
                for s in range(1, SEGS):
                    acc = jnp.where(lane_seg == s, chunk[s * 8 : s * 8 + 8], acc)
                chunks.append(acc)
            halves.append(chunks)
        for u in range(8):
            rows = jnp.concatenate([halves[0][u], halves[1][u]], axis=0).astype(BF)
            out_ref[(t * 8 + u) * 16 : (t * 8 + u) * 16 + 16, :] = rows


def spectra_of(got):
    vmem = pl.BlockSpec(memory_space=pltpu.VMEM)
    return pl.pallas_call(
        spectra_kernel,
        out_shape=jax.ShapeDtypeStruct((1024, 128), BF),
        in_specs=[vmem] + [pl.BlockSpec(memory_space=pl.ANY)] * 5,
        out_specs=vmem,
        scratch_shapes=[
            pltpu.VMEM((512, 512), BF),
            pltpu.VMEM(smooth_tables()[0].shape, BF),
            pltpu.VMEM((2, HALF), F32),
            pltpu.VMEM((128, 1024), BF),
            pltpu.VMEM((4, 4, NT // 4, 256), BF),
            pltpu.VMEM((64, NT), F32),
            pltpu.VMEM((4, 64, NT // 4), BF),
            pltpu.VMEM((2, 8, 64, 128), F32),
            pltpu.VMEM((2, 8, 64, 128), F32),
            pltpu.VMEM((2, 8, 128, 128), BF),
            pltpu.SemaphoreType.DMA((4,)),
            pltpu.SemaphoreType.DMA((4,)),
        ],
        compiler_params=pltpu.CompilerParams(vmem_limit_bytes=58 * 2**20),
        cost_estimate=pl.CostEstimate(flops=2**30, bytes_accessed=NT * NT // 2, transcendentals=0),
        name="spectra",
    )(got, parting_table(), smooth_tables()[0], taper_rows(), spread_table(), dft_table())


CHUNKS = 4


def pair_kernel(pos_ref, a_hbm, *refs):
    nrow, ncol = 8, 16
    b_hbm = refs[:nrow]
    lag_hbm, turn_ref, out_hbm, a_ref, b_ref, lag_ref, x_ref, y_ref, f_ref, o_ref, in_sem, lag_sem, out_sem = refs[nrow:]
    size = 1024 // CHUNKS

    def arrive(k):
        rows = pl.ds(k * size, size)
        copies = [pltpu.make_async_copy(a_hbm.at[:, rows, :], a_ref.at[:, rows, :], in_sem.at[k, nrow])]
        for r in range(nrow):
            copies.append(
                pltpu.make_async_copy(
                    b_hbm[r].at[rows, :], b_ref.at[pos_ref[2 + r], rows, :], in_sem.at[k, r]))
        return copies

    for k in range(CHUNKS):
        for copy in arrive(k):
            copy.start()
    lag_copy = pltpu.make_async_copy(lag_hbm, lag_ref, lag_sem)
    lag_copy.start()

    sub = lax.broadcasted_iota(jnp.int32, (16, 128), 0)
    lane = lax.broadcasted_iota(jnp.int32, (16, 128), 1)
    diagonal = (lane % GRP == sub).astype(F32).astype(BF)
    first = (lane // CH) % 2 == 0
    swap_sign = jnp.where(sub % 8 < 4, 1.0, -1.0)

    def group(g, special):
        rows = pl.ds(pl.multiple_of(g * 16, 16), 16)
        tiles = [a_ref[d, rows, :] for d in range(ncol)]
        turned = []
        for d in range(ncol):
            v = tiles[d].astype(F32)
            v = jnp.concatenate([pltpu.roll(v[0:8], 4, 0), pltpu.roll(v[8:16], 4, 0)], axis=0)
            turned.append(v * swap_sign)
        own = [b_ref[d, rows, :].astype(F32) for d in range(nrow)]
        prods = []
        for h in range(2):
            left = jnp.concatenate([t.astype(F32)[h * 8 : h * 8 + 8] for t in tiles], axis=0)
            right = jnp.concatenate([t[h * 8 : h * 8 + 8] for t in turned], axis=0)
            w = jnp.concatenate([left, right], axis=1).astype(BF)
            blocks = []
            for d in range(nrow):
                for c in range(CH):
                    r = h * 8 + c
                    re = jnp.broadcast_to(own[d][r : r + 1, :], (16, 128)).astype(BF)
                    im = jnp.broadcast_to(own[d][r + CH : r + CH + 1, :], (16, 128)).astype(BF)
                    blocks.append(jnp.concatenate([re * diagonal, im * diagonal], axis=1))
            lhs = jnp.concatenate(blocks, axis=0)
            prods.append(
                lax.dot_general(lhs, w, (((1,), (1,)), ((), ())), preferred_element_type=F32)
            )
        pairs = nrow * CH // 2
        for jp in range(pairs):
            parts = []
            for h in range(2):
                j = jp // 8 * 16 + jp % 8
                t0 = prods[h][j * 16 : j * 16 + 16]
                t1 = prods[h][(j + 8) * 16 : (j + 8) * 16 + 16]
                re = jnp.where(first, t0, pltpu.roll(t1, 4, 1))
                im = jnp.where(first, pltpu.roll(t0, 124, 1), t1)
                parts += [re, im]
            re0, im0, re1, im1 = parts
            sums = [re0 + re1, im0 - im1, re0 - re1, im0 + im1]
            if special:
                top = sub == 0
                sums = [
                    jnp.where(top, re0, sums[0]),
                    jnp.where(top, re1, sums[1]),
                    jnp.where(top, re0, sums[2]),
                    jnp.where(top, im1, sums[3]),
                ]
            for k in range(4):
                x_ref[k, rows, jp * 128 : jp * 128 + 128] = sums[k].astype(BF)

    @pl.loop(0, CHUNKS)
    def _(k):
        for copy in arrive(k):
            copy.wait()

        for u in range(NGRP // CHUNKS):
            group(k * (NGRP // CHUNKS) + u, False)

    group(0, True)
    lag_copy.wait()

    my_row, my_col = pos_ref[0], pos_ref[1]
    line = lax.broadcasted_iota(jnp.int32, (16, 128), 0)
    place = lax.broadcasted_iota(jnp.int32, (LAG_ROWS, 1), 0)
    alternate = jnp.where(place % 2 == 0, 1.0, -1.0)

    def leave(half, d):
        lines = pl.ds(half * 16, 16)
        return pltpu.make_async_copy(
            o_ref.at[pl.ds(d * CH, CH), lines, :], out_hbm.at[pl.ds(d * CH, CH), lines, :], out_sem.at[half, d])

    for half in range(2):

        @pl.loop(0, 4, unroll=4)
        def _(n):
            cols = pl.ds(pl.multiple_of(half * 1024 + n * 256, 256), 256)
            for odd in range(2):
                size = 256 if odd else LAG_ROWS
                cos = jnp.dot(lag_ref[2 * odd, :size], x_ref[2 * odd, :, cols], preferred_element_type=F32)
                sin = jnp.dot(lag_ref[2 * odd + 1, :size], x_ref[2 * odd + 1, :, cols], preferred_element_type=F32)
                if not odd:
                    cos += alternate * x_ref[1, 0:16, cols].astype(F32)[0:1]
                later = (cos + sin)[:256]
                sooner = cos - sin
                turned = jnp.dot(turn_ref[odd], sooner[:256].astype(BF), preferred_element_type=F32)
                for k in range(2):
                    half_cols = slice(k * 128, k * 128 + 128)
                    y_ref[k, pl.ds(odd, 256, stride=2), :] = turned[:, half_cols]
                    y_ref[k, pl.ds(LAGS // 2 + odd, 256, stride=2), :] = later[:, half_cols]
                    if not odd:
                        y_ref[k, 0:1, :] = sooner[256:257, half_cols]
            for k in range(2):
                at = pl.ds((n * 2 + k) * 129, 128)
                for t in range(LAGS // 128):
                    f_ref[t, at, :] = jnp.transpose(y_ref[k, t * 128 : t * 128 + 128, :])

        @pl.loop(0, ncol)
        def _(d):
            for c in range(CH):
                own = jnp.where(d == my_col, my_row * CH + c, -1)
                drop = line + half * 16 == own
                for t in range(LAGS // 128):
                    v = jnp.concatenate(
                        [f_ref[t, pl.ds(d * 8 + e * 4 + c, 8, stride=129), :] for e in range(2)], axis=0)
                    v = jnp.where(drop, 0.0, v * (1.0 / math.sqrt(SEGS * NF)))
                    o_ref[d * CH + c, half * 16 : half * 16 + 16, t * 128 : t * 128 + 128] = v.astype(BF)
            leave(half, d).start()

    for half in range(2):
        for d in range(ncol):
            leave(half, d).wait()


def pairs_of(pos, a, b):
    nrow, ncol = len(b), a.shape[0]
    assert nrow == 8 and ncol == 16
    anywhere = pl.BlockSpec(memory_space=pl.ANY)
    return pl.pallas_call(
        pair_kernel,
        out_shape=jax.ShapeDtypeStruct((ncol * CH, nrow * CH, LAGS), BF),
        in_specs=[pl.BlockSpec(memory_space=pltpu.SMEM)] + [anywhere] * (nrow + 2)
        + [pl.BlockSpec(memory_space=pltpu.VMEM)],
        out_specs=anywhere,
        scratch_shapes=[
            pltpu.VMEM((ncol, 1024, 128), BF),
            pltpu.VMEM((nrow, 1024, 128), BF),
            pltpu.VMEM((4, LAG_ROWS, HALF), BF),
            pltpu.VMEM((4, HALF, 2048), BF),
            pltpu.VMEM((2, LAGS, 128), F32),
            pltpu.VMEM((LAGS // 128, 8 * 129 + 8, 128), F32),
            pltpu.VMEM((ncol * CH, nrow * CH, LAGS), BF),
            pltpu.SemaphoreType.DMA((CHUNKS, nrow + 1)),
            pltpu.SemaphoreType.DMA,
            pltpu.SemaphoreType.DMA((2, ncol)),
        ],
        compiler_params=pltpu.CompilerParams(vmem_limit_bytes=60 * 2**20),
        cost_estimate=pl.CostEstimate(flops=2**34, bytes_accessed=16 * 2**20, transcendentals=0),
        name="pairs",
    )(pos, a, *b, lag_tables(), turning_tables())


def over_row(own, my_row):
    def move(block, step, across=0):
        pairs = [(y * 4 + z, (y ^ across) * 4 + (z + step) % 4) for y in range(2) for z in range(4)]
        return lax.ppermute(block, "row", pairs)

    y, z = my_row // 4, my_row % 4
    index = lambda step, across: (y ^ across) * 4 + (z + step) % 4
    other = move(own, 0, 1)
    left, right = move(own, 1), move(own, -1)
    other_left, other_right = move(other, 1), move(other, -1)
    far, other_far = move(left, 1), move(other_right, -1)
    blocks = [own, other, left, right, other_left, other_right, far, other_far]
    rows = [
        index(0, 0), index(0, 1), index(-1, 0), index(1, 0),
        index(-1, 1), index(1, 1), index(2, 0), index(2, 1),
    ]
    return blocks, rows


def local(strain, file_channels, file_counts, window_start):
    nrow, ncol = lax.axis_size("row"), lax.axis_size("col")
    my_row, my_col = lax.axis_index("row"), lax.axis_index("col")
    window = lax.dynamic_slice_in_dim(strain, window_start[0], WIN, 1)
    slot = jnp.arange(SLOTS, dtype=jnp.int32)
    live = slot < file_counts[0]
    owner = jnp.where(live, file_channels // CH // ncol, -1)
    place = file_channels % CH
    before = (owner[None, :] == owner[:, None]) & (slot[None, :] < slot[:, None])
    rank = jnp.sum(before.astype(jnp.int32), axis=1)
    lines = jnp.arange(2 * nrow, dtype=jnp.int32)
    choose = (owner[None, :] == lines[:, None] // 2) & (rank[None, :] == lines[:, None] % 2)
    labels = jnp.sum(jnp.where(choose, place[None, :] + 1, 0), axis=1) - 1
    bundle = jnp.dot(choose.astype(BF), window, preferred_element_type=F32).astype(BF)
    tags = jnp.broadcast_to(labels.astype(BF)[:, None], (2 * nrow, 128))
    sent = jnp.concatenate([bundle, tags], axis=1).reshape(nrow, 2, WIN + 128)
    got = lax.all_to_all(sent, "row", 0, 0).reshape(2 * nrow, WIN + 128)
    own = spectra_of(got)
    a = lax.all_gather(own, "col", axis=0)
    b, rows = over_row(own, my_row)
    pos = jnp.stack([my_row, my_col, *rows]).astype(jnp.int32)
    return pairs_of(pos, a, b)


def solution(mesh):
    placed = (P(("row", "col"), None), P(("row", "col")), P(("row", "col")), P(("row", "col")))
    return jax.shard_map(
        local, mesh=mesh, in_specs=placed, out_specs=P("row", "col", None), check_vma=False
    )
```
